32 devices in a mesh: ctx: 16 (over z, x, core), head: 2 (over y).
Axes of the slice: x: 2, y: 2, z: 4, core: 2. Of those that a mesh axis runs over, the one named last changes fastest.
Arguments:
- queries: bfloat16 [2048, 512], P('ctx', 'head'), may hold values from -6 to 6
- key_rows: bfloat16 [2048, 128], P('ctx'), may hold values from -6 to 6
- value_rows: bfloat16 [2048, 128], P('ctx'), may hold values from -6 to 6
- out_grad: bfloat16 [2048, 512], P('ctx', 'head'), may hold values from -6 to 6
- doc_lengths: int32 [8], replicated, may hold values from 1 to 1024, 2048 in all
- span_order: int32 [16, 2], replicated, may hold values from 0 to 31, as said below
Outputs:
- query_grad: bfloat16 [2048, 512], P('ctx', 'head')
- key_grad: bfloat16 [2048, 128], P(('ctx', 'head'))
- value_grad: bfloat16 [2048, 128], P(('ctx', 'head'))
The draws below stay inside these ranges and needn't reach their ends.
Inputs may be any that keep to these rules, and one draw needn't show every extreme that they name: `doc_lengths`: the lengths sum to 2048; the longest is exactly 1024. `span_order`: row i holds a span number c and its mirror 32 - 1 - c, in that order; the first entries of all rows are distinct.
All inputs are finite; a program needn't handle non-finite values.
Results may differ from the reference program's by a relative error of at most 0.025.
Values may be sent and summed in bfloat16 or wider, within the bound.
No kernel may reach another device: no remote copies, remote signals or barrier semaphores. Data moves between devices by JAX's collectives and lax.ppermute only.
A program may use at most 64 MiB of HBM per device.

```python
import math
import jax
import jax.numpy as jnp
import numpy as np
from jax import lax

HD = 128
QHEADS = 4
NDOCS = 8
SPAN = 64
NCHUNK = 32
TOKENS = 2048


def draw_queries(key, part):
    width = QHEADS * HD
    base = jnp.clip(jax.random.normal(jax.random.fold_in(key, 14), (TOKENS, width), jnp.float32), -6.0, 6.0)
    return base.astype(jnp.bfloat16)


def draw_key_rows(key, part):
    base = jnp.clip(jax.random.normal(jax.random.fold_in(key, 24), (TOKENS, HD), jnp.float32), -6.0, 6.0)
    return base.astype(jnp.bfloat16)


def draw_span_order(key, part):
    first = jax.random.permutation(jax.random.fold_in(key, 31), NCHUNK // 2)
    return jnp.stack([first, NCHUNK - 1 - first], axis=1).astype(jnp.int32)


def block_levels(rng, extent, shards, least, high):
    def one(axis_at, parts):
        draws = jax.random.uniform(jax.random.fold_in(jax.random.fold_in(rng, 6), axis_at), (parts,), jnp.float32, least / len(shards), high / len(shards))
        return jnp.repeat(jnp.exp(draws), extent[axis_at] // parts).reshape((-1,) + (1,) * (len(extent) - axis_at - 1))

    loudness = one(*shards[0])
    for cut in shards[1:]:
        loudness = loudness * one(*cut)
    return loudness


def length_profile(count, total, bound, lean):
    portions = [(1 << 20) // math.isqrt(standing ** lean) + 1 for standing in range(2, count + 1)]
    surplus, given = total - bound - (count - 1), [1] * (count - 1)
    while surplus > 0:
        free = [i for i in range(count - 1) if given[i] < bound]
        whole, budget = sum([portions[i] for i in free]), surplus
        for i in free:
            more = min(bound - given[i], max(1, budget * portions[i] // whole), surplus)
            given[i] = given[i] + more
            surplus = surplus - more
    return np.array([bound] + given)


def ragged_sizes(stream_key, amount, total, bound, lean):
    if amount == 2:
        one = jax.random.randint(stream_key, (), max(1, total - bound), min(bound, total - 1) + 1)
        return jnp.stack([one, total - one])
    lengths = jnp.asarray(length_profile(amount, total, bound, lean), jnp.int32)
    pairs = (amount - 1) // 2
    giver, receiver = lengths[1:1 + 2 * pairs:2], lengths[2:2 + 2 * pairs:2]
    room = jnp.minimum(giver - 1, bound - receiver)
    passed = jax.random.randint(jax.random.fold_in(stream_key, 1), (pairs,), 0, 1 << 20) % (room + 1)
    lengths = lengths.at[1:1 + 2 * pairs:2].set(giver - passed).at[2:2 + 2 * pairs:2].set(receiver + passed)
    return lengths[jax.random.permutation(jax.random.fold_in(stream_key, 2), amount)]


def scatter_about(rng, extent, scale, reach, cuts=(), held_as=jnp.bfloat16):
    result = jax.random.normal(rng, extent, jnp.float32) * scale
    if len(cuts) > 0:
        result = block_levels(rng, extent, cuts, -0.22, 0.18) * result
    return jnp.clip(result, min=-reach, max=reach).astype(held_as)


def setup_inputs(seed: int = 0) -> dict:
    keys = jax.random.split(jax.random.key(seed), 7)
    return {
        "queries": draw_queries(jax.random.fold_in(keys[6], 71), 0),
        "key_rows": draw_key_rows(jax.random.fold_in(keys[6], 71), 0),
        "value_rows": scatter_about(keys[2], (TOKENS, HD), 1.0, 6.0, ((0, 16),)),
        "out_grad": scatter_about(keys[3], (TOKENS, QHEADS * HD), 1.0, 6.0, ((0, 16), (1, 2))),
        "doc_lengths": ragged_sizes(keys[4], NDOCS, TOKENS, TOKENS // 2, 2).astype(jnp.int32),
        "span_order": draw_span_order(jax.random.fold_in(keys[6], 71), 0),
    }


def reference(queries, key_rows, value_rows, out_grad, doc_lengths, span_order):
    scaling = HD ** -0.5
    positions = (span_order.reshape(-1)[:, None] * SPAN + jnp.arange(SPAN, dtype=jnp.int32)[None, :]).reshape(-1).astype(jnp.int32)
    starts = jnp.cumsum(doc_lengths) - doc_lengths
    documents = jnp.sum((starts[None, :] <= positions[:, None]).astype(jnp.int32), axis=1) - 1
    keys_wide = key_rows.astype(jnp.float32)
    values_wide = value_rows.astype(jnp.float32)
    block_rows = min(256, TOKENS)
    block_count = TOKENS // block_rows
    query_blocks = queries.reshape(block_count, block_rows, QHEADS, HD)
    grad_blocks = out_grad.reshape(block_count, block_rows, QHEADS, HD)
    pos_blocks = positions.reshape(block_count, block_rows)
    doc_blocks = documents.reshape(block_count, block_rows)

    def one_block(carry, inputs):
        key_total, value_total = carry
        query_block, grad_block, pos_block, doc_block = inputs
        query_wide = query_block.astype(jnp.float32)
        grad_wide = grad_block.astype(jnp.float32)
        scores = jnp.einsum("qhd,kd->hqk", query_wide, keys_wide) * scaling
        allowed = (doc_block[:, None] == documents[None, :]) & (positions[None, :] <= pos_block[:, None])
        masked = jnp.where(allowed[None], scores, -1e30)
        row_max = jnp.max(masked, axis=-1, keepdims=True)
        row_total = jnp.sum(jnp.where(allowed[None], jnp.exp(masked - row_max), 0.0), axis=-1, keepdims=True)
        log_total = row_max + jnp.log(row_total)
        weights = jnp.where(allowed[None], jnp.exp(masked - log_total), 0.0)
        dprobs = jnp.einsum("qhd,kd->hqk", grad_wide, values_wide)
        row_delta = jnp.sum(weights * dprobs, axis=-1, keepdims=True)
        weights_low = weights.astype(jnp.bfloat16)
        dscores = (weights * (dprobs - row_delta)).astype(jnp.bfloat16)
        value_total = value_total + jnp.einsum("hqk,qhd->kd", weights_low.astype(jnp.float32), grad_wide)
        key_total = key_total + jnp.einsum("hqk,qhd->kd", dscores.astype(jnp.float32), query_wide) * scaling
        query_grad = (jnp.einsum("hqk,kd->qhd", dscores.astype(jnp.float32), keys_wide) * scaling).astype(jnp.bfloat16)
        return (key_total, value_total), query_grad

    zeros = jnp.zeros((TOKENS, HD), jnp.float32)
    (key_total, value_total), query_grad = lax.scan(one_block, (zeros, zeros), (query_blocks, grad_blocks, pos_blocks, doc_blocks))
    return query_grad.reshape(TOKENS, QHEADS * HD), key_total.astype(jnp.bfloat16), value_total.astype(jnp.bfloat16)
```

```python
import functools

import jax
import jax.numpy as jnp
from jax import lax
from jax.experimental import pallas as pl
from jax.experimental.pallas import tpu as pltpu
from jax.sharding import PartitionSpec as P

masked_value = -1e30
log2_e = 1.4426950408889634
GROUP = 4

NT = (((1,), (1,)), ((), ()))
NN = (((1,), (0,)), ((), ()))
TN = (((0,), (0,)), ((), ()))


def dot(a, b, dims):
    return lax.dot_general(a, b, dims, preferred_element_type=jnp.float32)


def span_positions(order_ref, index, shape, dim):
    rows = shape[dim]
    half = rows // 2
    at = lax.broadcasted_iota(jnp.int32, shape, dim)
    first = order_ref[index, 0] * half
    second = order_ref[index, 1] * half - half
    return at + jnp.where(at < half, first, second)


def document_start(lengths_ref, pos):
    start = jnp.int32(0)
    result = jnp.zeros_like(pos)
    for d in range(lengths_ref.shape[0]):
        result = jnp.where(pos >= start, start, result)
        start = start + lengths_ref[d]
    return result


def key_positions(order_ref, index, chunks, rows):
    base, member = index // GROUP, index % GROUP
    return [
        span_positions(order_ref, (base ^ b) * GROUP + member, (rows, 1), 0) for b in range(chunks)
    ]


def allowed_keys(lengths_ref, order_ref, index, j, key_pos, rows):
    owner = (index // GROUP) * GROUP + ((index % GROUP) ^ j)
    pos = span_positions(order_ref, owner, (1, rows), 1)
    first = document_start(lengths_ref, pos)
    return (key_pos <= pos) & (key_pos >= first)


def stats_kernel(chunks, heads, index_ref, lengths_ref, order_ref, *refs):
    group, chunk, out_ref = refs[:GROUP], refs[GROUP : GROUP + chunks], refs[-1]
    rows, width = chunk[0].shape
    hd = width // 2
    index = index_ref[0]
    factor = hd ** (-0.5) * log2_e
    keys = jnp.concatenate([c[:, :hd] for c in chunk], axis=0)
    values = jnp.concatenate([c[:, hd:] for c in chunk], axis=0)
    key_pos = jnp.concatenate(key_positions(order_ref, index, chunks, rows), axis=0)
    for j in range(GROUP):
        allowed = allowed_keys(lengths_ref, order_ref, index, j, key_pos, rows)
        for h in range(heads):
            query = group[j][:, h * hd : (h + 1) * hd]
            grad = group[j][:, (heads + h) * hd : (heads + h + 1) * hd]
            scores = jnp.where(allowed, dot(keys, query, NT) * factor, masked_value)
            dprobs = dot(values, grad, NT)
            top = jnp.max(scores, axis=0, keepdims=True)
            expo = jnp.exp2(scores - top)
            at = pl.ds((j * heads + h) * rows, rows)
            out_ref[0:1, at] = top
            out_ref[1:2, at] = jnp.sum(expo, axis=0, keepdims=True)
            out_ref[2:3, at] = jnp.sum(expo * dprobs, axis=0, keepdims=True)


def backward_kernel(chunks, heads, shards, index_ref, lengths_ref, order_ref, *refs):
    group, chunk = refs[:GROUP], refs[GROUP : GROUP + chunks]
    stats = refs[GROUP + chunks : 2 * GROUP + chunks]
    dq_ref, dkv_ref, dv_total, dk_total = refs[2 * GROUP + chunks :]
    rows, width = chunk[0].shape
    hd = width // 2
    index, shard = index_ref[0], index_ref[1]
    scaling = hd ** (-0.5)
    factor = scaling * log2_e
    keys = jnp.concatenate([c[:, :hd] for c in chunk], axis=0)
    values = jnp.concatenate([c[:, hd:] for c in chunk], axis=0)
    key_pos = jnp.concatenate(key_positions(order_ref, index, chunks, rows), axis=0)
    for j in range(GROUP):
        allowed = allowed_keys(lengths_ref, order_ref, index, j, key_pos, rows)
        for h in range(heads):
            query = group[j][:, h * hd : (h + 1) * hd]
            grad = group[j][:, (heads + h) * hd : (heads + h + 1) * hd]
            parts = [
                s[0:3, pl.ds(((j ^ t) * heads + h) * rows, rows)] for t, s in enumerate(stats)
            ]
            top = functools.reduce(jnp.maximum, [p[0:1] for p in parts])
            weight = [jnp.exp2(p[0:1] - top) for p in parts]
            total = sum(w * p[1:2] for w, p in zip(weight, parts))
            delta = sum(w * p[2:3] for w, p in zip(weight, parts)) / total
            log_total = top + jnp.log2(total)
            scores = jnp.where(allowed, dot(keys, query, NT) * factor, masked_value)
            weights = jnp.exp2(scores - log_total)
            dprobs = dot(values, grad, NT)
            weights_low = weights.astype(jnp.bfloat16)
            dscores = (weights * (dprobs - delta)).astype(jnp.bfloat16)
            dv = dot(weights_low, grad, NN)
            dk = dot(dscores, query, NN)
            if j == 0 and h == 0:
                dv_total[...] = dv
                dk_total[...] = dk
            else:
                dv_total[...] += dv
                dk_total[...] += dk
            dq = dot(dscores, keys, TN) * scaling
            dq_ref[pl.ds(j * rows, rows), h * hd : (h + 1) * hd] = dq.astype(jnp.bfloat16)
    part = rows // shards
    for t in range(shards):
        owner = lax.rem(shard + t, shards)
        for b in range(chunks):
            at = pl.ds(pl.multiple_of(b * rows + owner * part, part), part)
            to = pl.ds(b * part, part)
            dkv_ref[t, to, :hd] = (dk_total[at, :] * scaling).astype(jnp.bfloat16)
            dkv_ref[t, to, hd:] = dv_total[at, :].astype(jnp.bfloat16)


def local(queries, key_rows, value_rows, out_grad, doc_lengths, span_order):
    rows = queries.shape[0]
    hd = key_rows.shape[1]
    heads = queries.shape[1] // hd
    ctx_size, shards = lax.axis_size("ctx"), lax.axis_size("head")
    chunks = ctx_size // GROUP
    part = rows // shards
    index = jnp.stack([lax.axis_index("ctx"), lax.axis_index("head")]).astype(jnp.int32)

    def swap(x, bits):
        return lax.ppermute(x, "ctx", [(i, i ^ bits) for i in range(ctx_size)])

    def turn(x, by):
        return lax.ppermute(x, "head", [(i, (i + by) % shards) for i in range(shards)])

    packed_kv = jnp.concatenate([key_rows, value_rows], axis=1)
    packed_qg = jnp.concatenate([queries, out_grad], axis=1)
    chunk = [packed_kv] + [swap(packed_kv, b * GROUP) for b in range(1, chunks)]
    across = swap(packed_qg, 2)
    group = [packed_qg, swap(packed_qg, 1), across, swap(across, 1)]

    smem = pl.BlockSpec(memory_space=pltpu.SMEM)
    vmem = pl.BlockSpec(memory_space=pltpu.VMEM)
    params = pltpu.CompilerParams(vmem_limit_bytes=48 * 1024 * 1024)
    stats = pl.pallas_call(
        functools.partial(stats_kernel, chunks, heads),
        out_shape=jax.ShapeDtypeStruct((4, GROUP * heads * rows), jnp.float32),
        in_specs=[smem] * 3 + [vmem] * (GROUP + chunks),
        out_specs=vmem,
        compiler_params=params,
        name="stats",
    )(index, doc_lengths, span_order, *group, *chunk)
    all_stats = [stats] + [swap(stats, t) for t in range(1, GROUP)]

    dq, dkv = pl.pallas_call(
        functools.partial(backward_kernel, chunks, heads, shards),
        out_shape=(
            jax.ShapeDtypeStruct((GROUP * rows, heads * hd), jnp.bfloat16),
            jax.ShapeDtypeStruct((shards, chunks * part, 2 * hd), jnp.bfloat16),
        ),
        in_specs=[smem] * 3 + [vmem] * (2 * GROUP + chunks),
        out_specs=(vmem, vmem),
        scratch_shapes=[pltpu.VMEM((chunks * rows, hd), jnp.float32)] * 2,
        compiler_params=params,
        name="backward",
    )(index, doc_lengths, span_order, *group, *chunk, *all_stats)

    owned = dkv[0].astype(jnp.float32)
    for t in range(1, shards):
        owned = owned + turn(dkv[t], t).astype(jnp.float32)
    owned = owned.astype(jnp.bfloat16)
    total = owned[:part].astype(jnp.float32)
    for b in range(1, chunks):
        total = total + swap(owned[b * part : (b + 1) * part], b * GROUP).astype(jnp.float32)
    key_grad = total[:, :hd].astype(jnp.bfloat16)
    value_grad = total[:, hd:].astype(jnp.bfloat16)

    pair = dq[: 2 * rows].astype(jnp.float32) + swap(dq[2 * rows :], 2).astype(jnp.float32)
    pair = pair.astype(jnp.bfloat16)
    query_grad = pair[:rows].astype(jnp.float32) + swap(pair[rows:], 1).astype(jnp.float32)
    return (query_grad.astype(jnp.bfloat16), key_grad, value_grad)


def solution(mesh):
    in_specs = (P("ctx", "head"), P("ctx", None), P("ctx", None), P("ctx", "head"), P(), P())
    out_specs = (P("ctx", "head"), P(("ctx", "head"), None), P(("ctx", "head"), None))
    return jax.shard_map(local, mesh=mesh, in_specs=in_specs, out_specs=out_specs, check_vma=False)
```

```python
import functools

import jax
import jax.numpy as jnp
from jax import lax
from jax.experimental import pallas as pl
from jax.experimental.pallas import tpu as pltpu
from jax.sharding import PartitionSpec as P

masked_value = -1e30
log2_e = 1.4426950408889634
GROUP = 4

NT = (((1,), (1,)), ((), ()))
NN = (((1,), (0,)), ((), ()))
TN = (((0,), (0,)), ((), ()))


def dot(a, b, dims):
    return lax.dot_general(a, b, dims, preferred_element_type=jnp.float32)


def span_positions(order_ref, index, shape, dim):
    rows = shape[dim]
    half = rows // 2
    at = lax.broadcasted_iota(jnp.int32, shape, dim)
    first = order_ref[index, 0] * half
    second = order_ref[index, 1] * half - half
    return at + jnp.where(at < half, first, second)


def document_start(lengths_ref, pos):
    start = jnp.int32(0)
    result = jnp.zeros_like(pos)
    for d in range(lengths_ref.shape[0]):
        result = jnp.where(pos >= start, start, result)
        start = start + lengths_ref[d]
    return result


def key_positions(order_ref, index, chunks, rows):
    base, member = index // GROUP, index % GROUP
    return [
        span_positions(order_ref, (base ^ b) * GROUP + member, (rows, 1), 0) for b in range(chunks)
    ]


def allowed_keys(lengths_ref, order_ref, index, j, key_pos, rows):
    owner = (index // GROUP) * GROUP + ((index % GROUP) ^ j)
    pos = span_positions(order_ref, owner, (1, rows), 1)
    first = document_start(lengths_ref, pos)
    return (key_pos <= pos) & (key_pos >= first)


def stats_kernel(chunks, heads, index_ref, lengths_ref, order_ref, *refs):
    group, chunk, out_ref = refs[:GROUP], refs[GROUP : GROUP + chunks], refs[-1]
    rows, width = chunk[0].shape
    hd = width // 2
    index = index_ref[0]
    factor = hd ** (-0.5) * log2_e
    keys = jnp.concatenate([c[:, :hd] for c in chunk], axis=0)
    values = jnp.concatenate([c[:, hd:] for c in chunk], axis=0)
    key_pos = jnp.concatenate(key_positions(order_ref, index, chunks, rows), axis=0)
    for j in range(GROUP):
        allowed = allowed_keys(lengths_ref, order_ref, index, j, key_pos, rows)
        for h in range(heads):
            query = group[j][:, h * hd : (h + 1) * hd]
            grad = group[j][:, (heads + h) * hd : (heads + h + 1) * hd]
            scores = jnp.where(allowed, dot(keys, query, NT) * factor, masked_value)
            dprobs = dot(values, grad, NT)
            top = jnp.max(scores, axis=0, keepdims=True)
            expo = jnp.exp2(scores - top)
            at = pl.ds((j * heads + h) * rows, rows)
            out_ref[0:1, at] = top
            out_ref[1:2, at] = jnp.sum(expo, axis=0, keepdims=True)
            out_ref[2:3, at] = jnp.sum(expo * dprobs, axis=0, keepdims=True)


def backward_kernel(chunks, heads, shards, index_ref, lengths_ref, order_ref, *refs):
    group, chunk = refs[:GROUP], refs[GROUP : GROUP + chunks]
    stats = refs[GROUP + chunks : 2 * GROUP + chunks]
    dq_ref, dkv_ref, dv_total, dk_total = refs[2 * GROUP + chunks :]
    rows, width = chunk[0].shape
    hd = width // 2
    index, shard = index_ref[0], index_ref[1]
    scaling = hd ** (-0.5)
    factor = scaling * log2_e
    keys = jnp.concatenate([c[:, :hd] for c in chunk], axis=0)
    values = jnp.concatenate([c[:, hd:] for c in chunk], axis=0)
    key_pos = jnp.concatenate(key_positions(order_ref, index, chunks, rows), axis=0)
    for j in range(GROUP):
        allowed = allowed_keys(lengths_ref, order_ref, index, j, key_pos, rows)
        for h in range(heads):
            query = group[j][:, h * hd : (h + 1) * hd]
            grad = group[j][:, (heads + h) * hd : (heads + h + 1) * hd]
            parts = [
                s[0:3, pl.ds(((j ^ t) * heads + h) * rows, rows)] for t, s in enumerate(stats)
            ]
            top = functools.reduce(jnp.maximum, [p[0:1] for p in parts])
            weight = [jnp.exp2(p[0:1] - top) for p in parts]
            total = sum(w * p[1:2] for w, p in zip(weight, parts))
            delta = sum(w * p[2:3] for w, p in zip(weight, parts)) / total
            log_total = top + jnp.log2(total)
            scores = jnp.where(allowed, dot(keys, query, NT) * factor, masked_value)
            weights = jnp.exp2(scores - log_total)
            dprobs = dot(values, grad, NT)
            weights_low = weights.astype(jnp.bfloat16)
            dscores = (weights * (dprobs - delta)).astype(jnp.bfloat16)
            dv = dot(weights_low, grad, NN)
            dk = dot(dscores, query, NN)
            if j == 0 and h == 0:
                dv_total[...] = dv
                dk_total[...] = dk
            else:
                dv_total[...] += dv
                dk_total[...] += dk
            dq = dot(dscores, keys, TN) * scaling
            dq_ref[pl.ds(j * rows, rows), h * hd : (h + 1) * hd] = dq.astype(jnp.bfloat16)
    part = rows // shards
    for t in range(shards):
        owner = lax.rem(shard + t, shards)
        for b in range(chunks):
            at = pl.ds(pl.multiple_of(b * rows + owner * part, part), part)
            to = pl.ds(b * part, part)
            dkv_ref[t, to, :hd] = (dk_total[at, :] * scaling).astype(jnp.bfloat16)
            dkv_ref[t, to, hd:] = dv_total[at, :].astype(jnp.bfloat16)


def local(queries, key_rows, value_rows, out_grad, doc_lengths, span_order):
    rows = queries.shape[0]
    hd = key_rows.shape[1]
    heads = queries.shape[1] // hd
    ctx_size, shards = lax.axis_size("ctx"), lax.axis_size("head")
    chunks = ctx_size // GROUP
    part = rows // shards
    index = jnp.stack([lax.axis_index("ctx"), lax.axis_index("head")]).astype(jnp.int32)

    def swap(x, bits):
        return lax.ppermute(x, "ctx", [(i, i ^ bits) for i in range(ctx_size)])

    def turn(x, by):
        return lax.ppermute(x, "head", [(i, (i + by) % shards) for i in range(shards)])

    packed_kv = jnp.concatenate([key_rows, value_rows], axis=1)
    packed_qg = jnp.concatenate([queries, out_grad], axis=1)
    chunk = [packed_kv] + [swap(packed_kv, b * GROUP) for b in range(1, chunks)]
    group = [packed_qg] + [swap(packed_qg, t) for t in range(1, GROUP)]

    smem = pl.BlockSpec(memory_space=pltpu.SMEM)
    vmem = pl.BlockSpec(memory_space=pltpu.VMEM)
    params = pltpu.CompilerParams(vmem_limit_bytes=48 * 1024 * 1024)
    stats = pl.pallas_call(
        functools.partial(stats_kernel, chunks, heads),
        out_shape=jax.ShapeDtypeStruct((4, GROUP * heads * rows), jnp.float32),
        in_specs=[smem] * 3 + [vmem] * (GROUP + chunks),
        out_specs=vmem,
        compiler_params=params,
        name="stats",
    )(index, doc_lengths, span_order, *group, *chunk)
    all_stats = [stats] + [swap(stats, t) for t in range(1, GROUP)]

    dq, dkv = pl.pallas_call(
        functools.partial(backward_kernel, chunks, heads, shards),
        out_shape=(
            jax.ShapeDtypeStruct((GROUP * rows, heads * hd), jnp.bfloat16),
            jax.ShapeDtypeStruct((shards, chunks * part, 2 * hd), jnp.bfloat16),
        ),
        in_specs=[smem] * 3 + [vmem] * (2 * GROUP + chunks),
        out_specs=(vmem, vmem),
        scratch_shapes=[pltpu.VMEM((chunks * rows, hd), jnp.float32)] * 2,
        compiler_params=params,
        name="backward",
    )(index, doc_lengths, span_order, *group, *chunk, *all_stats)

    owned = dkv[0].astype(jnp.float32)
    for t in range(1, shards):
        owned = owned + turn(dkv[t], t).astype(jnp.float32)
    owned = owned.astype(jnp.bfloat16)
    total = owned[:part].astype(jnp.float32)
    for b in range(1, chunks):
        total = total + swap(owned[b * part : (b + 1) * part], b * GROUP).astype(jnp.float32)
    key_grad = total[:, :hd].astype(jnp.bfloat16)
    value_grad = total[:, hd:].astype(jnp.bfloat16)

    pair = dq[: 2 * rows].astype(jnp.float32) + swap(dq[2 * rows :], 2).astype(jnp.float32)
    pair = pair.astype(jnp.bfloat16)
    query_grad = pair[:rows].astype(jnp.float32) + swap(pair[rows:], 1).astype(jnp.float32)
    return (query_grad.astype(jnp.bfloat16), key_grad, value_grad)


def solution(mesh):
    in_specs = (P("ctx", "head"), P("ctx", None), P("ctx", None), P("ctx", "head"), P(), P())
    out_specs = (P("ctx", "head"), P(("ctx", "head"), None), P(("ctx", "head"), None))
    return jax.shard_map(local, mesh=mesh, in_specs=in_specs, out_specs=out_specs, check_vma=False)
```

```python
import functools

import jax
import jax.numpy as jnp
from jax import lax
from jax.experimental import pallas as pl
from jax.experimental.pallas import tpu as pltpu
from jax.sharding import PartitionSpec as P

masked_value = -1e30
log2_e = 1.4426950408889634
GROUP = 4

NT = (((1,), (1,)), ((), ()))
NN = (((1,), (0,)), ((), ()))


def dot(a, b, dims):
    return lax.dot_general(a, b, dims, preferred_element_type=jnp.float32)


def offsets(size):
    group = (0, 1, 2, 3)
    return group, tuple(range(0, size, 4))


def place_kernel(group, chunk, lengths, order, place_ref):
    rows = place_ref.shape[1]
    index = lax.axis_index("ctx")
    half = rows // 2
    at = lax.broadcasted_iota(jnp.int32, (1, rows), 1)
    for j, bits in enumerate(group):
        first = order[0, index ^ bits] * half
        second = order[1, index ^ bits] * half - half
        pos = at + jnp.where(at < half, first, second)
        start = jnp.int32(0)
        opens = jnp.zeros_like(pos)
        for d in range(lengths.shape[0]):
            opens = jnp.where(pos >= start, start, opens)
            start = start + lengths[d]
        place_ref[j : j + 1, :] = pos
        place_ref[GROUP + j : GROUP + j + 1, :] = opens
    for b, bits in enumerate(chunk):
        for h in range(2):
            to = 2 * GROUP + 2 * b + h
            place_ref[to : to + 1, :] = jnp.full((1, rows), order[h, index ^ bits] * half)


def both_heads(ref, heads, at):
    hd = ref.shape[1] // (2 * heads)
    return jnp.concatenate(
        [ref[:, (at + h) * hd : (at + h + 1) * hd] for h in range(heads)], axis=0
    )


def stats_kernel(chunks, heads, place_ref, *refs):
    group, chunk = refs[:GROUP], refs[GROUP : GROUP + chunks]
    out_ref, expo_ref, dprobs_ref = refs[GROUP + chunks :]
    rows, width = chunk[0].shape
    hd = width // 2
    factor = hd ** (-0.5) * log2_e
    keys = jnp.concatenate([c[:, :hd] for c in chunk], axis=0)
    values = jnp.concatenate([c[:, hd:] for c in chunk], axis=0)
    at = lax.broadcasted_iota(jnp.int32, (rows // 2, rows), 0)
    key_pos = jnp.concatenate(
        [at + place_ref[2 * GROUP + s : 2 * GROUP + s + 1, :] for s in range(2 * chunks)], axis=0
    )
    for j in range(GROUP):
        pos, opens = place_ref[j : j + 1, :], place_ref[GROUP + j : GROUP + j + 1, :]
        allowed = (key_pos <= pos) & (key_pos >= opens)
        bias = jnp.where(allowed, 0.0, masked_value)
        bias = jnp.concatenate([bias] * heads, axis=1)
        scores = dot(keys, both_heads(group[j], heads, 0), NT) * factor + bias
        dprobs = dot(values, both_heads(group[j], heads, heads), NT)
        top = jnp.max(scores, axis=0, keepdims=True)
        expo = jnp.exp2(scores - top)
        at = pl.ds(j * heads * rows, heads * rows)
        out_ref[0:1, at] = top
        out_ref[1:2, at] = jnp.sum(expo, axis=0, keepdims=True)
        out_ref[2:3, at] = jnp.sum(expo * dprobs, axis=0, keepdims=True)
        expo_ref[:, at] = expo
        dprobs_ref[:, at] = dprobs


def backward_kernel(chunks, heads, shards, *refs):
    group, chunk = refs[:GROUP], refs[GROUP : GROUP + chunks]
    stats = refs[GROUP + chunks : 2 * GROUP + chunks]
    expo_ref, dprobs_ref, near_ref, far_ref = refs[2 * GROUP + chunks : 2 * GROUP + chunks + 4]
    outs = refs[2 * GROUP + chunks + 4 : -2]
    dv_total, dk_total = refs[-2:]
    rows, width = chunk[0].shape
    hd = width // 2
    shard = lax.axis_index("head")
    scaling = hd ** (-0.5)
    keys = jnp.concatenate([c[:, :hd] for c in chunk], axis=0)
    keys_across = keys.T
    for j in range(GROUP):
        parts = [
            s[0:3, pl.ds((j ^ t) * heads * rows, heads * rows)] for t, s in enumerate(stats)
        ]
        top = functools.reduce(jnp.maximum, [p[0:1] for p in parts])
        weight = [jnp.exp2(p[0:1] - top) for p in parts]
        total = sum(w * p[1:2] for w, p in zip(weight, parts))
        delta = sum(w * p[2:3] for w, p in zip(weight, parts)) / total
        own = weight[0] / total
        at = pl.ds(j * heads * rows, heads * rows)
        weights = expo_ref[:, at] * own
        weights_low = weights.astype(jnp.bfloat16)
        dscores = (weights * (dprobs_ref[:, at] - delta)).astype(jnp.bfloat16)
        dv = dot(weights_low, both_heads(group[j], heads, heads), NN)
        dk = dot(dscores, both_heads(group[j], heads, 0), NN)
        if j == 0:
            dv_total[...] = dv
            dk_total[...] = dk
        else:
            dv_total[...] += dv
            dk_total[...] += dk
        dq = ((dot(keys_across, dscores, NN) * scaling).T).astype(jnp.bfloat16)
        half = GROUP // 2
        to = (near_ref, far_ref)[j // half]
        for h in range(heads):
            to[pl.ds(j % half * rows, rows), h * hd : (h + 1) * hd] = dq[h * rows : (h + 1) * rows]
    part = rows // shards
    for t in range(shards):
        owner = lax.rem(shard + t, shards)
        for b in range(chunks):
            at = pl.ds(pl.multiple_of(b * rows + owner * part, part), part)
            to = pl.ds(b * part, part)
            outs[t][to, :hd] = (dk_total[at, :] * scaling).astype(jnp.bfloat16)
            outs[t][to, hd:] = dv_total[at, :].astype(jnp.bfloat16)


def finish_kernel(chunks, owned_ref, *refs):
    came, (pair_ref, other_ref) = refs[: chunks - 1], refs[chunks - 1 : chunks + 1]
    query_ref, key_ref, value_ref = refs[chunks + 1 :]
    part, hd = key_ref.shape
    rows = query_ref.shape[0]
    total = owned_ref[:part].astype(jnp.float32)
    for ref in came:
        total = total + ref[...].astype(jnp.float32)
    key_ref[...] = total[:, :hd].astype(jnp.bfloat16)
    value_ref[...] = total[:, hd:].astype(jnp.bfloat16)
    query = pair_ref[:rows].astype(jnp.float32) + other_ref[...].astype(jnp.float32)
    query_ref[...] = query.astype(jnp.bfloat16)


def local(queries, key_rows, value_rows, out_grad, doc_lengths, span_order):
    rows, width = queries.shape
    hd = key_rows.shape[1]
    heads = width // hd
    ctx_size, shards = lax.axis_size("ctx"), lax.axis_size("head")
    chunks = ctx_size // GROUP
    part = rows // shards
    group_bits, chunk_bits = offsets(ctx_size)

    def swap(x, bits):
        return lax.ppermute(x, "ctx", [(i, i ^ bits) for i in range(ctx_size)])

    def turn(x, by):
        return lax.ppermute(x, "head", [(i, (i + by) % shards) for i in range(shards)])

    vmem = pl.BlockSpec(memory_space=pltpu.VMEM)
    params = pltpu.CompilerParams(vmem_limit_bytes=40 * 1024 * 1024)
    small = pltpu.CompilerParams(vmem_limit_bytes=4 * 1024 * 1024)

    def array(shape, dtype=jnp.bfloat16):
        return jax.ShapeDtypeStruct(shape, dtype)

    place = pl.pallas_call(
        functools.partial(place_kernel, group_bits, chunk_bits),
        out_shape=array((2 * (GROUP + chunks), rows), jnp.int32),
        in_specs=[pl.BlockSpec(memory_space=pltpu.SMEM)] * 2,
        out_specs=vmem,
        compiler_params=small,
        name="place",
    )(doc_lengths, span_order.T)

    packed_kv = jnp.concatenate([key_rows, value_rows], axis=1)
    packed_qg = jnp.concatenate([queries, out_grad], axis=1)
    chunk = [packed_kv] + [swap(packed_kv, bits) for bits in chunk_bits[1:]]
    group = [packed_qg] + [swap(packed_qg, bits) for bits in group_bits[1:]]

    square = array((chunks * rows, GROUP * heads * rows), jnp.float32)
    stats, expo, dprobs = pl.pallas_call(
        functools.partial(stats_kernel, chunks, heads),
        out_shape=(array((4, GROUP * heads * rows), jnp.float32), square, square),
        in_specs=[vmem] * (1 + GROUP + chunks),
        out_specs=(vmem, vmem, vmem),
        compiler_params=params,
        name="stats",
    )(place, *group, *chunk)
    all_stats = [stats] + [swap(stats, bits) for bits in group_bits[1:]]

    half = array((GROUP // 2 * rows, width))
    piece = array((chunks * part, 2 * hd))
    near, far, *dkv = pl.pallas_call(
        functools.partial(backward_kernel, chunks, heads, shards),
        out_shape=(half, half) + (piece,) * shards,
        in_specs=[vmem] * (2 * GROUP + chunks + 2),
        out_specs=(vmem,) * (2 + shards),
        scratch_shapes=[pltpu.VMEM((chunks * rows, hd), jnp.float32)] * 2,
        compiler_params=params,
        name="backward",
    )(*group, *chunk, *all_stats, expo, dprobs)

    owned = dkv[0].astype(jnp.float32)
    for t in range(1, shards):
        owned = owned + turn(dkv[t], t).astype(jnp.float32)
    owned = owned.astype(jnp.bfloat16)
    came = [
        swap(owned[b * part : (b + 1) * part], chunk_bits[b]) for b in range(1, chunks)
    ]
    pair = (near.astype(jnp.float32) + swap(far, group_bits[2]).astype(jnp.float32)).astype(jnp.bfloat16)
    other = swap(pair[rows:], group_bits[1])
    return tuple(
        pl.pallas_call(
            functools.partial(finish_kernel, chunks),
            out_shape=(array((rows, width)), array((part, hd)), array((part, hd))),
            in_specs=[vmem] * (chunks + 2),
            out_specs=(vmem, vmem, vmem),
            compiler_params=small,
            name="finish",
        )(owned, *came, pair, other)
    )


def solution(mesh):
    in_specs = (P("ctx", "head"), P("ctx", None), P("ctx", None), P("ctx", "head"), P(), P())
    out_specs = (P("ctx", "head"), P(("ctx", "head"), None), P(("ctx", "head"), None))
    return jax.shard_map(local, mesh=mesh, in_specs=in_specs, out_specs=out_specs, check_vma=False)
```

```python
import functools

import jax
import jax.numpy as jnp
from jax import lax
from jax.experimental import pallas as pl
from jax.experimental.pallas import tpu as pltpu
from jax.sharding import PartitionSpec as P

masked_value = -1e30
log2_e = 1.4426950408889634
GROUP = 4

NT = (((1,), (1,)), ((), ()))
NN = (((1,), (0,)), ((), ()))


def dot(a, b, dims):
    return lax.dot_general(a, b, dims, preferred_element_type=jnp.float32)


def offsets(size):
    group = (0, 1, 2, 3)
    return group, tuple(range(0, size, 4))


def place_kernel(group, chunk, lengths, order, place_ref):
    rows = place_ref.shape[1]
    index = lax.axis_index("ctx")
    half = rows // 2
    at = lax.broadcasted_iota(jnp.int32, (1, rows), 1)
    for j, bits in enumerate(group):
        first = order[0, index ^ bits] * half
        second = order[1, index ^ bits] * half - half
        pos = at + jnp.where(at < half, first, second)
        start = jnp.int32(0)
        opens = jnp.zeros_like(pos)
        for d in range(lengths.shape[0]):
            opens = jnp.where(pos >= start, start, opens)
            start = start + lengths[d]
        place_ref[j : j + 1, :] = pos
        place_ref[GROUP + j : GROUP + j + 1, :] = opens
    for b, bits in enumerate(chunk):
        for h in range(2):
            to = 2 * GROUP + 2 * b + h
            place_ref[to : to + 1, :] = jnp.full((1, rows), order[h, index ^ bits] * half)


def both_heads(ref, heads, which):
    rows, hd = ref.shape[0] // 2, ref.shape[1] // heads
    at = pl.ds(which * rows, rows)
    return jnp.concatenate([ref[at, h * hd : (h + 1) * hd] for h in range(heads)], axis=0)


def stats_kernel(chunks, heads, place_ref, *refs):
    group, chunk = refs[:GROUP], refs[GROUP : GROUP + chunks]
    out_ref, expo_ref, dprobs_ref = refs[GROUP + chunks :]
    rows, width = chunk[0].shape
    hd = width // 2
    factor = hd ** (-0.5) * log2_e
    keys = jnp.concatenate([c[:, :hd] for c in chunk], axis=0)
    values = jnp.concatenate([c[:, hd:] for c in chunk], axis=0)
    at = lax.broadcasted_iota(jnp.int32, (rows // 2, rows), 0)
    key_pos = jnp.concatenate(
        [at + place_ref[2 * GROUP + s : 2 * GROUP + s + 1, :] for s in range(2 * chunks)], axis=0
    )
    for j in range(GROUP):
        pos, opens = place_ref[j : j + 1, :], place_ref[GROUP + j : GROUP + j + 1, :]
        allowed = (key_pos <= pos) & (key_pos >= opens)
        bias = jnp.where(allowed, 0.0, masked_value)
        bias = jnp.concatenate([bias] * heads, axis=1)
        scores = dot(keys, both_heads(group[j], heads, 0), NT) * factor + bias
        dprobs = dot(values, both_heads(group[j], heads, 1), NT)
        top = jnp.max(scores, axis=0, keepdims=True)
        expo = jnp.exp2(scores - top)
        at = pl.ds(j * heads * rows, heads * rows)
        out_ref[0:1, at] = top
        out_ref[1:2, at] = jnp.sum(expo, axis=0, keepdims=True)
        out_ref[2:3, at] = jnp.sum(expo * dprobs, axis=0, keepdims=True)
        expo_ref[:, at] = expo
        dprobs_ref[:, at] = dprobs


def backward_kernel(chunks, heads, shards, *refs):
    group, chunk = refs[:GROUP], refs[GROUP : GROUP + chunks]
    stats = refs[GROUP + chunks : 2 * GROUP + chunks]
    expo_ref, dprobs_ref, near_ref, far_ref = refs[2 * GROUP + chunks : 2 * GROUP + chunks + 4]
    outs = refs[2 * GROUP + chunks + 4 : -2]
    dv_total, dk_total = refs[-2:]
    rows, width = chunk[0].shape
    hd = width // 2
    shard = lax.axis_index("head")
    scaling = hd ** (-0.5)
    keys = jnp.concatenate([c[:, :hd] for c in chunk], axis=0)
    keys_across = keys.T
    for j in range(GROUP):
        parts = [
            s[0:3, pl.ds((j ^ t) * heads * rows, heads * rows)] for t, s in enumerate(stats)
        ]
        top = functools.reduce(jnp.maximum, [p[0:1] for p in parts])
        weight = [jnp.exp2(p[0:1] - top) for p in parts]
        total = sum(w * p[1:2] for w, p in zip(weight, parts))
        delta = sum(w * p[2:3] for w, p in zip(weight, parts)) / total
        own = weight[0] / total
        at = pl.ds(j * heads * rows, heads * rows)
        weights = expo_ref[:, at] * own
        weights_low = weights.astype(jnp.bfloat16)
        dscores = (weights * (dprobs_ref[:, at] - delta)).astype(jnp.bfloat16)
        dv = dot(weights_low, both_heads(group[j], heads, 1), NN)
        dk = dot(dscores, both_heads(group[j], heads, 0), NN)
        if j == 0:
            dv_total[...] = dv
            dk_total[...] = dk
        else:
            dv_total[...] += dv
            dk_total[...] += dk
        dq = ((dot(keys_across, dscores, NN) * scaling).T).astype(jnp.bfloat16)
        half = GROUP // 2
        to = (near_ref, far_ref)[j // half]
        for h in range(heads):
            to[pl.ds(j % half * rows, rows), h * hd : (h + 1) * hd] = dq[h * rows : (h + 1) * rows]
    part = rows // shards
    for t in range(shards):
        owner = lax.rem(shard + t, shards)
        for b in range(chunks):
            at = pl.ds(pl.multiple_of(b * rows + owner * part, part), part)
            to = pl.ds(b * part, part)
            outs[t][to, :hd] = (dk_total[at, :] * scaling).astype(jnp.bfloat16)
            outs[t][to, hd:] = dv_total[at, :].astype(jnp.bfloat16)


def finish_kernel(chunks, owned_ref, *refs):
    came, (pair_ref, other_ref) = refs[: chunks - 1], refs[chunks - 1 : chunks + 1]
    query_ref, key_ref, value_ref = refs[chunks + 1 :]
    part, hd = key_ref.shape
    rows = query_ref.shape[0]
    total = owned_ref[:part].astype(jnp.float32)
    for ref in came:
        total = total + ref[...].astype(jnp.float32)
    key_ref[...] = total[:, :hd].astype(jnp.bfloat16)
    value_ref[...] = total[:, hd:].astype(jnp.bfloat16)
    query = pair_ref[:rows].astype(jnp.float32) + other_ref[...].astype(jnp.float32)
    query_ref[...] = query.astype(jnp.bfloat16)


def local(queries, key_rows, value_rows, out_grad, doc_lengths, span_order):
    rows, width = queries.shape
    hd = key_rows.shape[1]
    heads = width // hd
    ctx_size, shards = lax.axis_size("ctx"), lax.axis_size("head")
    chunks = ctx_size // GROUP
    part = rows // shards
    group_bits, chunk_bits = offsets(ctx_size)

    def swap(x, bits):
        return lax.ppermute(x, "ctx", [(i, i ^ bits) for i in range(ctx_size)])

    def turn(x, by):
        return lax.ppermute(x, "head", [(i, (i + by) % shards) for i in range(shards)])

    vmem = pl.BlockSpec(memory_space=pltpu.VMEM)
    params = pltpu.CompilerParams(vmem_limit_bytes=40 * 1024 * 1024)
    small = pltpu.CompilerParams(vmem_limit_bytes=4 * 1024 * 1024)

    def array(shape, dtype=jnp.bfloat16):
        return jax.ShapeDtypeStruct(shape, dtype)

    place = pl.pallas_call(
        functools.partial(place_kernel, group_bits, chunk_bits),
        out_shape=array((2 * (GROUP + chunks), rows), jnp.int32),
        in_specs=[pl.BlockSpec(memory_space=pltpu.SMEM)] * 2,
        out_specs=vmem,
        compiler_params=small,
        name="place",
    )(doc_lengths, span_order.T)

    packed = jnp.concatenate(
        [jnp.concatenate([key_rows, value_rows], axis=1), queries, out_grad], axis=0
    )
    packed = lax.optimization_barrier(packed)
    packed_kv, packed_qg = packed[:rows], packed[rows:]
    chunk = [packed_kv] + [swap(packed_kv, bits) for bits in chunk_bits[1:]]
    group = [packed_qg] + [swap(packed_qg, bits) for bits in group_bits[1:]]

    square = array((chunks * rows, GROUP * heads * rows), jnp.float32)
    stats, expo, dprobs = pl.pallas_call(
        functools.partial(stats_kernel, chunks, heads),
        out_shape=(array((4, GROUP * heads * rows), jnp.float32), square, square),
        in_specs=[vmem] * (1 + GROUP + chunks),
        out_specs=(vmem, vmem, vmem),
        compiler_params=params,
        name="stats",
    )(place, *group, *chunk)
    all_stats = [stats] + [swap(stats, bits) for bits in group_bits[1:]]

    half = array((GROUP // 2 * rows, width))
    piece = array((chunks * part, 2 * hd))
    near, far, *dkv = pl.pallas_call(
        functools.partial(backward_kernel, chunks, heads, shards),
        out_shape=(half, half) + (piece,) * shards,
        in_specs=[vmem] * (2 * GROUP + chunks + 2),
        out_specs=(vmem,) * (2 + shards),
        scratch_shapes=[pltpu.VMEM((chunks * rows, hd), jnp.float32)] * 2,
        compiler_params=params,
        name="backward",
    )(*group, *chunk, *all_stats, expo, dprobs)

    owned = dkv[0].astype(jnp.float32)
    for t in range(1, shards):
        owned = owned + turn(dkv[t], t).astype(jnp.float32)
    owned = owned.astype(jnp.bfloat16)
    came = [
        swap(owned[b * part : (b + 1) * part], chunk_bits[b]) for b in range(1, chunks)
    ]
    pair = (near.astype(jnp.float32) + swap(far, group_bits[2]).astype(jnp.float32)).astype(jnp.bfloat16)
    other = swap(pair[rows:], group_bits[1])
    return tuple(
        pl.pallas_call(
            functools.partial(finish_kernel, chunks),
            out_shape=(array((rows, width)), array((part, hd)), array((part, hd))),
            in_specs=[vmem] * (chunks + 2),
            out_specs=(vmem, vmem, vmem),
            compiler_params=small,
            name="finish",
        )(owned, *came, pair, other)
    )


def solution(mesh):
    in_specs = (P("ctx", "head"), P("ctx", None), P("ctx", None), P("ctx", "head"), P(), P())
    out_specs = (P("ctx", "head"), P(("ctx", "head"), None), P(("ctx", "head"), None))
    return jax.shard_map(local, mesh=mesh, in_specs=in_specs, out_specs=out_specs, check_vma=False)
```

```python
import functools

import jax
import jax.numpy as jnp
from jax import lax
from jax.experimental import pallas as pl
from jax.experimental.pallas import tpu as pltpu
from jax.sharding import PartitionSpec as P

masked_value = -1e30
log2_e = 1.4426950408889634
GROUP = 4

NT = (((1,), (1,)), ((), ()))
NN = (((1,), (0,)), ((), ()))


def dot(a, b, dims):
    return lax.dot_general(a, b, dims, preferred_element_type=jnp.float32)


def offsets(size):
    group = (0, 1, 2, 3)
    return group, tuple(range(0, size, 4))


def place_kernel(group, chunk, docs, ints, place_ref):
    rows = place_ref.shape[1]
    count = (ints.shape[0] - docs) // 2
    index = lax.axis_index("ctx")
    half = rows // 2
    at = lax.broadcasted_iota(jnp.int32, (1, rows), 1)
    for j, bits in enumerate(group):
        first = ints[docs + (index ^ bits)] * half
        second = ints[docs + count + (index ^ bits)] * half - half
        pos = at + jnp.where(at < half, first, second)
        start = jnp.int32(0)
        opens = jnp.zeros_like(pos)
        for d in range(docs):
            opens = jnp.where(pos >= start, start, opens)
            start = start + ints[d]
        place_ref[j : j + 1, :] = pos
        place_ref[GROUP + j : GROUP + j + 1, :] = opens
    for b, bits in enumerate(chunk):
        for h in range(2):
            to = 2 * GROUP + 2 * b + h
            base = ints[docs + h * count + (index ^ bits)] * half
            place_ref[to : to + 1, :] = jnp.full((1, rows), base)


def both_heads(ref, heads, which):
    rows, hd = ref.shape[0] // 2, ref.shape[1] // heads
    at = pl.ds(which * rows, rows)
    return jnp.concatenate([ref[at, h * hd : (h + 1) * hd] for h in range(heads)], axis=0)


def stats_kernel(chunks, heads, place_ref, *refs):
    group, chunk = refs[:GROUP], refs[GROUP : GROUP + chunks]
    out_ref, top_ref, expo_ref, dprobs_ref = refs[GROUP + chunks :]
    group = (*group[:-1], group[-1].at[1 - lax.axis_index("ctx") % 2])
    rows, width = chunk[0].shape
    hd = width // 2
    factor = hd ** (-0.5) * log2_e
    keys = jnp.concatenate([c[:, :hd] for c in chunk], axis=0)
    values = jnp.concatenate([c[:, hd:] for c in chunk], axis=0)
    at = lax.broadcasted_iota(jnp.int32, (rows // 2, rows), 0)
    key_pos = jnp.concatenate(
        [at + place_ref[2 * GROUP + s : 2 * GROUP + s + 1, :] for s in range(2 * chunks)], axis=0
    )
    for j in range(GROUP):
        pos, opens = place_ref[j : j + 1, :], place_ref[GROUP + j : GROUP + j + 1, :]
        allowed = (key_pos <= pos) & (key_pos >= opens)
        bias = jnp.where(allowed, 0.0, masked_value)
        bias = jnp.concatenate([bias] * heads, axis=1)
        scores = dot(keys, both_heads(group[j], heads, 0), NT) * factor + bias
        dprobs = dot(values, both_heads(group[j], heads, 1), NT)
        top = jnp.max(scores, axis=0, keepdims=True)
        expo = jnp.exp2(scores - top)
        total = jnp.sum(expo, axis=0, keepdims=True)
        at = pl.ds(j * heads * rows, heads * rows)
        out_ref[0:1, at] = top + jnp.log2(total)
        out_ref[1:2, at] = jnp.sum(expo * dprobs, axis=0, keepdims=True) / total
        top_ref[0:1, at] = top
        expo_ref[:, at] = expo
        dprobs_ref[:, at] = dprobs


def backward_kernel(chunks, heads, shards, *refs):
    group, chunk = refs[:GROUP], refs[GROUP : GROUP + chunks]
    stats = refs[GROUP + chunks : 2 * GROUP + chunks]
    top_ref, expo_ref, dprobs_ref, near_ref, far_ref = refs[2 * GROUP + chunks :][:5]
    outs = refs[2 * GROUP + chunks + 5 : -2]
    dv_total, dk_total = refs[-2:]
    group = (*group[:-1], group[-1].at[1 - lax.axis_index("ctx") % 2])
    rows, width = chunk[0].shape
    hd = width // 2
    shard = lax.axis_index("head")
    scaling = hd ** (-0.5)
    keys = jnp.concatenate([c[:, :hd] for c in chunk], axis=0)
    keys_across = keys.T
    for j in range(GROUP):
        at = pl.ds(j * heads * rows, heads * rows)
        parts = [
            s[0:2, pl.ds((j ^ t) * heads * rows, heads * rows)] for t, s in enumerate(stats)
        ]
        largest = functools.reduce(jnp.maximum, [p[0:1] for p in parts])
        share = [jnp.exp2(p[0:1] - largest) for p in parts]
        total = sum(share)
        delta = sum(w * p[1:2] for w, p in zip(share, parts)) / total
        own = jnp.exp2(top_ref[0:1, at] - largest) / total
        weights = expo_ref[:, at] * own
        weights_low = weights.astype(jnp.bfloat16)
        dscores = (weights * (dprobs_ref[:, at] - delta)).astype(jnp.bfloat16)
        dv = dot(weights_low, both_heads(group[j], heads, 1), NN)
        dk = dot(dscores, both_heads(group[j], heads, 0), NN)
        if j == 0:
            dv_total[...] = dv
            dk_total[...] = dk
        else:
            dv_total[...] += dv
            dk_total[...] += dk
        dq = ((dot(keys_across, dscores, NN) * scaling).T).astype(jnp.bfloat16)
        half = GROUP // 2
        to = (near_ref, far_ref)[j % half]
        for h in range(heads):
            to[pl.ds(j // half * rows, rows), h * hd : (h + 1) * hd] = dq[h * rows : (h + 1) * rows]
    part = rows // shards
    for t in range(shards):
        owner = lax.rem(shard + t, shards)
        for b in range(chunks):
            at = pl.ds(pl.multiple_of(b * rows + owner * part, part), part)
            to = pl.ds(b * part, part)
            outs[t][to, :hd] = (dk_total[at, :] * scaling).astype(jnp.bfloat16)
            outs[t][to, hd:] = dv_total[at, :].astype(jnp.bfloat16)


def finish_kernel(chunks, owned_ref, *refs):
    came, (pair_ref, other_ref) = refs[: chunks - 1], refs[chunks - 1 : chunks + 1]
    query_ref, key_ref, value_ref = refs[chunks + 1 :]
    part, hd = key_ref.shape
    rows = query_ref.shape[0]
    total = owned_ref[:part].astype(jnp.float32)
    for ref in came:
        total = total + ref[...].astype(jnp.float32)
    key_ref[...] = total[:, :hd].astype(jnp.bfloat16)
    value_ref[...] = total[:, hd:].astype(jnp.bfloat16)
    query = pair_ref[:rows].astype(jnp.float32) + other_ref[...].astype(jnp.float32)
    query_ref[...] = query.astype(jnp.bfloat16)


def local(queries, key_rows, value_rows, out_grad, doc_lengths, span_order):
    rows, width = queries.shape
    hd = key_rows.shape[1]
    heads = width // hd
    ctx_size, shards = lax.axis_size("ctx"), lax.axis_size("head")
    chunks = ctx_size // GROUP
    part = rows // shards
    group_bits, chunk_bits = offsets(ctx_size)

    def swap(x, bits):
        return lax.ppermute(x, "ctx", [(i, i ^ bits) for i in range(ctx_size)])

    def turn(x, by):
        return lax.ppermute(x, "head", [(i, (i + by) % shards) for i in range(shards)])

    vmem = pl.BlockSpec(memory_space=pltpu.VMEM)
    params = pltpu.CompilerParams(vmem_limit_bytes=40 * 1024 * 1024)
    small = pltpu.CompilerParams(vmem_limit_bytes=4 * 1024 * 1024)

    def array(shape, dtype=jnp.bfloat16):
        return jax.ShapeDtypeStruct(shape, dtype)

    place = pl.pallas_call(
        functools.partial(place_kernel, group_bits, chunk_bits, doc_lengths.shape[0]),
        out_shape=array((2 * (GROUP + chunks), rows), jnp.int32),
        in_specs=[pl.BlockSpec(memory_space=pltpu.SMEM)],
        out_specs=vmem,
        compiler_params=small,
        name="place",
    )(jnp.concatenate([doc_lengths, span_order.T.reshape(-1)]))

    packed = jnp.concatenate(
        [jnp.concatenate([key_rows, value_rows], axis=1), queries, out_grad], axis=0
    )
    packed = lax.optimization_barrier(packed)
    packed_kv, packed_qg = packed[:rows], packed[rows:]
    chunk = [packed_kv] + [swap(packed_kv, bits) for bits in chunk_bits[1:]]
    across = swap(packed_qg, group_bits[2])
    beside = swap(packed_qg, group_bits[1])
    pairs = [[i, i + 1] for i in range(0, ctx_size, 2)]
    both = lax.all_gather(across, "ctx", axis_index_groups=pairs)
    group = [packed_qg, beside, across, both]

    square = array((chunks * rows, GROUP * heads * rows), jnp.float32)
    stats, top, expo, dprobs = pl.pallas_call(
        functools.partial(stats_kernel, chunks, heads),
        out_shape=(
            array((2, GROUP * heads * rows), jnp.float32),
            array((1, GROUP * heads * rows), jnp.float32),
            square,
            square,
        ),
        in_specs=[vmem] * (1 + GROUP + chunks),
        out_specs=(vmem, vmem, vmem, vmem),
        compiler_params=params,
        name="stats",
    )(place, *group, *chunk)
    all_stats = [stats] + [swap(stats, bits) for bits in group_bits[1:]]

    half = array((GROUP // 2 * rows, width))
    piece = array((chunks * part, 2 * hd))
    near, far, *dkv = pl.pallas_call(
        functools.partial(backward_kernel, chunks, heads, shards),
        out_shape=(half, half) + (piece,) * shards,
        in_specs=[vmem] * (2 * GROUP + chunks + 3),
        out_specs=(vmem,) * (2 + shards),
        scratch_shapes=[pltpu.VMEM((chunks * rows, hd), jnp.float32)] * 2,
        compiler_params=params,
        name="backward",
    )(*group, *chunk, *all_stats, top, expo, dprobs)

    owned = dkv[0].astype(jnp.float32)
    for t in range(1, shards):
        owned = owned + turn(dkv[t], t).astype(jnp.float32)
    owned = owned.astype(jnp.bfloat16)
    came = [
        swap(owned[b * part : (b + 1) * part], chunk_bits[b]) for b in range(1, chunks)
    ]
    pair = (near.astype(jnp.float32) + swap(far, group_bits[1]).astype(jnp.float32)).astype(jnp.bfloat16)
    other = swap(pair[rows:], group_bits[2])
    return tuple(
        pl.pallas_call(
            functools.partial(finish_kernel, chunks),
            out_shape=(array((rows, width)), array((part, hd)), array((part, hd))),
            in_specs=[vmem] * (chunks + 2),
            out_specs=(vmem, vmem, vmem),
            compiler_params=small,
            name="finish",
        )(owned, *came, pair, other)
    )


def solution(mesh):
    in_specs = (P("ctx", "head"), P("ctx", None), P("ctx", None), P("ctx", "head"), P(), P())
    out_specs = (P("ctx", "head"), P(("ctx", "head"), None), P(("ctx", "head"), None))
    return jax.shard_map(local, mesh=mesh, in_specs=in_specs, out_specs=out_specs, check_vma=False)
```

```python
import functools

import jax
import jax.numpy as jnp
from jax import lax
from jax.experimental import pallas as pl
from jax.experimental.pallas import tpu as pltpu
from jax.sharding import PartitionSpec as P

masked_value = -1e30
log2_e = 1.4426950408889634
GROUP = 4

NT = (((1,), (1,)), ((), ()))
NN = (((1,), (0,)), ((), ()))


def dot(a, b, dims):
    return lax.dot_general(a, b, dims, preferred_element_type=jnp.float32)


def offsets(size):
    group = (0, 1, 2, 3)
    return group, tuple(range(0, size, 4))


def place_kernel(group, chunk, docs, ints, place_ref):
    rows = place_ref.shape[1]
    count = (ints.shape[0] - docs) // 2
    index = lax.axis_index("ctx")
    half = rows // 2
    at = lax.broadcasted_iota(jnp.int32, (1, rows), 1)
    for j, bits in enumerate(group):
        first = ints[docs + (index ^ bits)] * half
        second = ints[docs + count + (index ^ bits)] * half - half
        pos = at + jnp.where(at < half, first, second)
        start = jnp.int32(0)
        opens = jnp.zeros_like(pos)
        for d in range(docs):
            opens = jnp.where(pos >= start, start, opens)
            start = start + ints[d]
        place_ref[j : j + 1, :] = pos
        place_ref[GROUP + j : GROUP + j + 1, :] = opens
    for b, bits in enumerate(chunk):
        for h in range(2):
            to = 2 * GROUP + 2 * b + h
            base = ints[docs + h * count + (index ^ bits)] * half
            place_ref[to : to + 1, :] = jnp.full((1, rows), base)


def both_heads(ref, heads, which):
    rows, hd = ref.shape[0] // 2, ref.shape[1] // heads
    at = pl.ds(which * rows, rows)
    return jnp.concatenate([ref[at, h * hd : (h + 1) * hd] for h in range(heads)], axis=0)


def stats_kernel(chunks, heads, place_ref, *refs):
    group, chunk = refs[:GROUP], refs[GROUP : GROUP + chunks]
    out_ref, top_ref, expo_ref, dprobs_ref = refs[GROUP + chunks :]
    rows, width = chunk[0].shape
    hd = width // 2
    factor = hd ** (-0.5) * log2_e
    keys = jnp.concatenate([c[:, :hd] for c in chunk], axis=0)
    values = jnp.concatenate([c[:, hd:] for c in chunk], axis=0)
    at = lax.broadcasted_iota(jnp.int32, (rows // 2, rows), 0)
    key_pos = jnp.concatenate(
        [at + place_ref[2 * GROUP + s : 2 * GROUP + s + 1, :] for s in range(2 * chunks)], axis=0
    )
    for j in range(GROUP):
        pos, opens = place_ref[j : j + 1, :], place_ref[GROUP + j : GROUP + j + 1, :]
        allowed = (key_pos <= pos) & (key_pos >= opens)
        bias = jnp.where(allowed, 0.0, masked_value)
        bias = jnp.concatenate([bias] * heads, axis=1)
        scores = dot(keys, both_heads(group[j], heads, 0), NT) * factor + bias
        dprobs = dot(values, both_heads(group[j], heads, 1), NT)
        top = jnp.max(scores, axis=0, keepdims=True)
        expo = jnp.exp2(scores - top)
        total = jnp.sum(expo, axis=0, keepdims=True)
        at = pl.ds(j * heads * rows, heads * rows)
        out_ref[0:1, at] = top + jnp.log2(total)
        out_ref[1:2, at] = jnp.sum(expo * dprobs, axis=0, keepdims=True) / total
        top_ref[0:1, at] = top
        expo_ref[:, at] = expo
        dprobs_ref[:, at] = dprobs


def backward_kernel(chunks, heads, shards, *refs):
    group, chunk = refs[:GROUP], refs[GROUP : GROUP + chunks]
    stats = refs[GROUP + chunks : 2 * GROUP + chunks]
    top_ref, expo_ref, dprobs_ref, near_ref, far_ref = refs[2 * GROUP + chunks :][:5]
    outs = refs[2 * GROUP + chunks + 5 : -2]
    dv_total, dk_total = refs[-2:]
    rows, width = chunk[0].shape
    hd = width // 2
    shard = lax.axis_index("head")
    scaling = hd ** (-0.5)
    keys = jnp.concatenate([c[:, :hd] for c in chunk], axis=0)
    keys_across = keys.T
    for j in range(GROUP):
        at = pl.ds(j * heads * rows, heads * rows)
        parts = [
            s[0:2, pl.ds((j ^ t) * heads * rows, heads * rows)] for t, s in enumerate(stats)
        ]
        largest = functools.reduce(jnp.maximum, [p[0:1] for p in parts])
        share = [jnp.exp2(p[0:1] - largest) for p in parts]
        total = sum(share)
        delta = sum(w * p[1:2] for w, p in zip(share, parts)) / total
        own = jnp.exp2(top_ref[0:1, at] - largest) / total
        weights = expo_ref[:, at] * own
        weights_low = weights.astype(jnp.bfloat16)
        dscores = (weights * (dprobs_ref[:, at] - delta)).astype(jnp.bfloat16)
        dv = dot(weights_low, both_heads(group[j], heads, 1), NN)
        dk = dot(dscores, both_heads(group[j], heads, 0), NN)
        if j == 0:
            dv_total[...] = dv
            dk_total[...] = dk
        else:
            dv_total[...] += dv
            dk_total[...] += dk
        dq = ((dot(keys_across, dscores, NN) * scaling).T).astype(jnp.bfloat16)
        half = GROUP // 2
        to = (near_ref, far_ref)[j % half]
        for h in range(heads):
            to[pl.ds(j // half * rows, rows), h * hd : (h + 1) * hd] = dq[h * rows : (h + 1) * rows]
    part = rows // shards
    for t in range(shards):
        owner = lax.rem(shard + t, shards)
        for b in range(chunks):
            at = pl.ds(pl.multiple_of(b * rows + owner * part, part), part)
            to = pl.ds(b * part, part)
            outs[t][to, :hd] = (dk_total[at, :] * scaling).astype(jnp.bfloat16)
            outs[t][to, hd:] = dv_total[at, :].astype(jnp.bfloat16)


def finish_kernel(chunks, owned_ref, *refs):
    came, (pair_ref, other_ref) = refs[: chunks - 1], refs[chunks - 1 : chunks + 1]
    query_ref, key_ref, value_ref = refs[chunks + 1 :]
    part, hd = key_ref.shape
    rows = query_ref.shape[0]
    total = owned_ref[:part].astype(jnp.float32)
    for ref in came:
        total = total + ref[...].astype(jnp.float32)
    key_ref[...] = total[:, :hd].astype(jnp.bfloat16)
    value_ref[...] = total[:, hd:].astype(jnp.bfloat16)
    query = pair_ref[:rows].astype(jnp.float32) + other_ref[...].astype(jnp.float32)
    query_ref[...] = query.astype(jnp.bfloat16)


def local(queries, key_rows, value_rows, out_grad, doc_lengths, span_order):
    rows, width = queries.shape
    hd = key_rows.shape[1]
    heads = width // hd
    ctx_size, shards = lax.axis_size("ctx"), lax.axis_size("head")
    chunks = ctx_size // GROUP
    part = rows // shards
    group_bits, chunk_bits = offsets(ctx_size)

    def swap(x, bits):
        return lax.ppermute(x, "ctx", [(i, i ^ bits) for i in range(ctx_size)])

    def turn(x, by):
        return lax.ppermute(x, "head", [(i, (i + by) % shards) for i in range(shards)])

    vmem = pl.BlockSpec(memory_space=pltpu.VMEM)
    params = pltpu.CompilerParams(vmem_limit_bytes=40 * 1024 * 1024)
    small = pltpu.CompilerParams(vmem_limit_bytes=4 * 1024 * 1024)

    def array(shape, dtype=jnp.bfloat16):
        return jax.ShapeDtypeStruct(shape, dtype)

    place = pl.pallas_call(
        functools.partial(place_kernel, group_bits, chunk_bits, doc_lengths.shape[0]),
        out_shape=array((2 * (GROUP + chunks), rows), jnp.int32),
        in_specs=[pl.BlockSpec(memory_space=pltpu.SMEM)],
        out_specs=vmem,
        compiler_params=small,
        cost_estimate=pl.CostEstimate(flops=1000000000, bytes_accessed=0, transcendentals=0),
        name="place",
    )(jnp.concatenate([doc_lengths, span_order.T.reshape(-1)]))

    packed = jnp.concatenate(
        [jnp.concatenate([key_rows, value_rows], axis=1), queries, out_grad], axis=0
    )
    packed = lax.optimization_barrier(packed)
    packed_kv, packed_qg = packed[:rows], packed[rows:]
    chunk = [packed_kv] + [swap(packed_kv, bits) for bits in chunk_bits[1:]]
    across = swap(packed_qg, group_bits[2])
    beside = swap(packed_qg, group_bits[1])
    group = [packed_qg, beside, across, swap(across, group_bits[1])]

    square = array((chunks * rows, GROUP * heads * rows), jnp.float32)
    stats, top, expo, dprobs = pl.pallas_call(
        functools.partial(stats_kernel, chunks, heads),
        out_shape=(
            array((2, GROUP * heads * rows), jnp.float32),
            array((1, GROUP * heads * rows), jnp.float32),
            square,
            square,
        ),
        in_specs=[vmem] * (1 + GROUP + chunks),
        out_specs=(vmem, vmem, vmem, vmem),
        compiler_params=params,
        name="stats",
    )(place, *group, *chunk)
    all_stats = [stats] + [swap(stats, bits) for bits in group_bits[1:]]

    half = array((GROUP // 2 * rows, width))
    piece = array((chunks * part, 2 * hd))
    near, far, *dkv = pl.pallas_call(
        functools.partial(backward_kernel, chunks, heads, shards),
        out_shape=(half, half) + (piece,) * shards,
        in_specs=[vmem] * (2 * GROUP + chunks + 3),
        out_specs=(vmem,) * (2 + shards),
        scratch_shapes=[pltpu.VMEM((chunks * rows, hd), jnp.float32)] * 2,
        compiler_params=params,
        name="backward",
    )(*group, *chunk, *all_stats, top, expo, dprobs)

    owned = dkv[0].astype(jnp.float32)
    for t in range(1, shards):
        owned = owned + turn(dkv[t], t).astype(jnp.float32)
    owned = owned.astype(jnp.bfloat16)
    came = [
        swap(owned[b * part : (b + 1) * part], chunk_bits[b]) for b in range(1, chunks)
    ]
    pair = (near.astype(jnp.float32) + swap(far, group_bits[1]).astype(jnp.float32)).astype(jnp.bfloat16)
    other = swap(pair[rows:], group_bits[2])
    return tuple(
        pl.pallas_call(
            functools.partial(finish_kernel, chunks),
            out_shape=(array((rows, width)), array((part, hd)), array((part, hd))),
            in_specs=[vmem] * (chunks + 2),
            out_specs=(vmem, vmem, vmem),
            compiler_params=small,
            name="finish",
        )(owned, *came, pair, other)
    )


def solution(mesh):
    in_specs = (P("ctx", "head"), P("ctx", None), P("ctx", None), P("ctx", "head"), P(), P())
    out_specs = (P("ctx", "head"), P(("ctx", "head"), None), P(("ctx", "head"), None))
    return jax.shard_map(local, mesh=mesh, in_specs=in_specs, out_specs=out_specs, check_vma=False)
```

```python
import functools

import jax
import jax.numpy as jnp
from jax import lax
from jax.experimental import pallas as pl
from jax.experimental.pallas import tpu as pltpu
from jax.sharding import PartitionSpec as P

masked_value = -1e30
log2_e = 1.4426950408889634
GROUP = 4

NT = (((1,), (1,)), ((), ()))
NN = (((1,), (0,)), ((), ()))


def dot(a, b, dims):
    return lax.dot_general(a, b, dims, preferred_element_type=jnp.float32)


def offsets(size):
    group = (0, 1, 2, 3)
    return group, tuple(range(0, size, 4))


def place_kernel(group, chunk, docs, ints, place_ref):
    rows = place_ref.shape[1]
    count = (ints.shape[0] - docs) // 2
    index = lax.axis_index("ctx")
    half = rows // 2
    at = lax.broadcasted_iota(jnp.int32, (1, rows), 1)
    for j, bits in enumerate(group):
        first = ints[docs + (index ^ bits)] * half
        second = ints[docs + count + (index ^ bits)] * half - half
        pos = at + jnp.where(at < half, first, second)
        start = jnp.int32(0)
        opens = jnp.zeros_like(pos)
        for d in range(docs):
            opens = jnp.where(pos >= start, start, opens)
            start = start + ints[d]
        place_ref[j : j + 1, :] = pos
        place_ref[GROUP + j : GROUP + j + 1, :] = opens
    for b, bits in enumerate(chunk):
        for h in range(2):
            to = 2 * GROUP + 2 * b + h
            base = ints[docs + h * count + (index ^ bits)] * half
            place_ref[to : to + 1, :] = jnp.full((1, rows), base)


def both_heads(ref, heads, which):
    rows, hd = ref.shape[0] // 2, ref.shape[1] // heads
    at = pl.ds(which * rows, rows)
    return jnp.concatenate([ref[at, h * hd : (h + 1) * hd] for h in range(heads)], axis=0)


def stats_kernel(chunks, heads, place_ref, *refs):
    group, chunk = refs[:GROUP], refs[GROUP : GROUP + chunks]
    out_ref, top_ref, expo_ref, dprobs_ref = refs[GROUP + chunks :]
    rows, width = chunk[0].shape
    hd = width // 2
    factor = hd ** (-0.5) * log2_e
    keys = jnp.concatenate([c[:, :hd] for c in chunk], axis=0)
    values = jnp.concatenate([c[:, hd:] for c in chunk], axis=0)
    at = lax.broadcasted_iota(jnp.int32, (rows // 2, rows), 0)
    key_pos = jnp.concatenate(
        [at + place_ref[2 * GROUP + s : 2 * GROUP + s + 1, :] for s in range(2 * chunks)], axis=0
    )
    for j in range(GROUP):
        pos, opens = place_ref[j : j + 1, :], place_ref[GROUP + j : GROUP + j + 1, :]
        allowed = (key_pos <= pos) & (key_pos >= opens)
        bias = jnp.where(allowed, 0.0, masked_value)
        bias = jnp.concatenate([bias] * heads, axis=1)
        scores = dot(keys, both_heads(group[j], heads, 0), NT) * factor + bias
        dprobs = dot(values, both_heads(group[j], heads, 1), NT)
        top = jnp.max(scores, axis=0, keepdims=True)
        expo = jnp.exp2(scores - top)
        total = jnp.sum(expo, axis=0, keepdims=True)
        at = pl.ds(j * heads * rows, heads * rows)
        out_ref[0:1, at] = top + jnp.log2(total)
        out_ref[1:2, at] = jnp.sum(expo * dprobs, axis=0, keepdims=True) / total
        top_ref[0:1, at] = top
        expo_ref[:, at] = expo
        dprobs_ref[:, at] = dprobs


def backward_kernel(chunks, heads, shards, *refs):
    group, chunk = refs[:GROUP], refs[GROUP : GROUP + chunks]
    stats = refs[GROUP + chunks : 2 * GROUP + chunks]
    top_ref, expo_ref, dprobs_ref, near_ref, far_ref = refs[2 * GROUP + chunks :][:5]
    outs = refs[2 * GROUP + chunks + 5 : -2]
    dv_total, dk_total = refs[-2:]
    rows, width = chunk[0].shape
    hd = width // 2
    shard = lax.axis_index("head")
    scaling = hd ** (-0.5)
    keys = jnp.concatenate([c[:, :hd] for c in chunk], axis=0)
    keys_across = keys.T
    for j in range(GROUP):
        at = pl.ds(j * heads * rows, heads * rows)
        parts = [
            s[0:2, pl.ds((j ^ t) * heads * rows, heads * rows)] for t, s in enumerate(stats)
        ]
        largest = functools.reduce(jnp.maximum, [p[0:1] for p in parts])
        share = [jnp.exp2(p[0:1] - largest) for p in parts]
        total = sum(share)
        delta = sum(w * p[1:2] for w, p in zip(share, parts)) / total
        own = jnp.exp2(top_ref[0:1, at] - largest) / total
        weights = expo_ref[:, at] * own
        weights_low = weights.astype(jnp.bfloat16)
        dscores = (weights * (dprobs_ref[:, at] - delta)).astype(jnp.bfloat16)
        dv = dot(weights_low, both_heads(group[j], heads, 1), NN)
        dk = dot(dscores, both_heads(group[j], heads, 0), NN)
        if j == 0:
            dv_total[...] = dv
            dk_total[...] = dk
        else:
            dv_total[...] += dv
            dk_total[...] += dk
        dq = ((dot(keys_across, dscores, NN) * scaling).T).astype(jnp.bfloat16)
        half = GROUP // 2
        to = (near_ref, far_ref)[j // half]
        for h in range(heads):
            to[pl.ds(j % half * rows, rows), h * hd : (h + 1) * hd] = dq[h * rows : (h + 1) * rows]
    part = rows // shards
    half = chunks // 2
    for t in range(shards):
        owner = lax.rem(shard + t, shards)
        for b in range(chunks):
            at = pl.ds(pl.multiple_of(b * rows + owner * part, part), part)
            if b < half:
                out, to = outs[b], pl.ds(t * part, part)
            else:
                out, to = outs[half + t], pl.ds((b - half) * part, part)
            out[to, :hd] = (dk_total[at, :] * scaling).astype(jnp.bfloat16)
            out[to, hd:] = dv_total[at, :].astype(jnp.bfloat16)


def fold_kernel(*refs):
    total = refs[0][...].astype(jnp.float32)
    for ref in refs[1:-1]:
        total = total + ref[...].astype(jnp.float32)
    refs[-1][...] = total.astype(jnp.bfloat16)


def finish_kernel(owned_ref, *refs):
    *came, key_ref, value_ref = refs
    part, hd = key_ref.shape
    total = owned_ref[:part].astype(jnp.float32)
    for ref in came:
        total = total + ref[...].astype(jnp.float32)
    key_ref[...] = total[:, :hd].astype(jnp.bfloat16)
    value_ref[...] = total[:, hd:].astype(jnp.bfloat16)


def query_sum_kernel(pair_ref, other_ref, query_ref):
    rows = query_ref.shape[0]
    query = pair_ref[:rows].astype(jnp.float32) + other_ref[...].astype(jnp.float32)
    query_ref[...] = query.astype(jnp.bfloat16)


def local(queries, key_rows, value_rows, out_grad, doc_lengths, span_order):
    rows, width = queries.shape
    hd = key_rows.shape[1]
    heads = width // hd
    ctx_size, shards = lax.axis_size("ctx"), lax.axis_size("head")
    chunks = ctx_size // GROUP
    part = rows // shards
    group_bits, chunk_bits = offsets(ctx_size)

    def swap(x, bits):
        return lax.ppermute(x, "ctx", [(i, i ^ bits) for i in range(ctx_size)])

    def turn(x, by):
        return lax.ppermute(x, "head", [(i, (i + by) % shards) for i in range(shards)])

    vmem = pl.BlockSpec(memory_space=pltpu.VMEM)
    params = pltpu.CompilerParams(vmem_limit_bytes=40 * 1024 * 1024)
    small = pltpu.CompilerParams(vmem_limit_bytes=4 * 1024 * 1024)

    def array(shape, dtype=jnp.bfloat16):
        return jax.ShapeDtypeStruct(shape, dtype)

    place = pl.pallas_call(
        functools.partial(place_kernel, group_bits, chunk_bits, doc_lengths.shape[0]),
        out_shape=array((2 * (GROUP + chunks), rows), jnp.int32),
        in_specs=[pl.BlockSpec(memory_space=pltpu.SMEM)],
        out_specs=vmem,
        compiler_params=small,
        cost_estimate=pl.CostEstimate(flops=1000000000, bytes_accessed=0, transcendentals=0),
        name="place",
    )(jnp.concatenate([doc_lengths, span_order.T.reshape(-1)]))

    packed = jnp.concatenate(
        [jnp.concatenate([key_rows, value_rows], axis=1), queries, out_grad], axis=0
    )
    packed = lax.optimization_barrier(packed)
    packed_kv, packed_qg = packed[:rows], packed[rows:]
    chunk = [packed_kv] + [swap(packed_kv, bits) for bits in chunk_bits[1:]]
    across = swap(packed_qg, group_bits[2])
    beside = swap(packed_qg, group_bits[1])
    group = [packed_qg, beside, across, swap(across, group_bits[1])]

    square = array((chunks * rows, GROUP * heads * rows), jnp.float32)
    stats, top, expo, dprobs = pl.pallas_call(
        functools.partial(stats_kernel, chunks, heads),
        out_shape=(
            array((2, GROUP * heads * rows), jnp.float32),
            array((1, GROUP * heads * rows), jnp.float32),
            square,
            square,
        ),
        in_specs=[vmem] * (1 + GROUP + chunks),
        out_specs=(vmem, vmem, vmem, vmem),
        compiler_params=params,
        name="stats",
    )(place, *group, *chunk)
    all_stats = [stats] + [swap(stats, bits) for bits in group_bits[1:]]

    pair_rows = array((GROUP // 2 * rows, width))
    half = chunks // 2
    pieces = (array((rows, 2 * hd)),) * half + (array((half * part, 2 * hd)),) * shards
    near, far, *dkv = pl.pallas_call(
        functools.partial(backward_kernel, chunks, heads, shards),
        out_shape=(pair_rows, pair_rows) + pieces,
        in_specs=[vmem] * (2 * GROUP + chunks + 3),
        out_specs=(vmem,) * (2 + len(pieces)),
        scratch_shapes=[pltpu.VMEM((chunks * rows, hd), jnp.float32)] * 2,
        compiler_params=params,
        name="backward",
    )(*group, *chunk, *all_stats, top, expo, dprobs)

    def fold(parts, flops):
        return pl.pallas_call(
            fold_kernel,
            out_shape=jax.ShapeDtypeStruct(parts[0].shape, jnp.bfloat16),
            in_specs=[vmem] * len(parts),
            out_specs=vmem,
            compiler_params=small,
            cost_estimate=pl.CostEstimate(flops=flops, bytes_accessed=0, transcendentals=0),
            name="fold",
        )(*parts)

    across = fold([dkv[half]] + [turn(dkv[half + t], t) for t in range(1, shards)], 0)
    owned = fold([dkv[0]] + [swap(dkv[b], chunk_bits[b]) for b in range(1, half)], 1000000000)
    came = [
        swap(across[k * part : (k + 1) * part], chunk_bits[half + k]) for k in range(half)
    ] + [turn(owned[t * part : (t + 1) * part], t) for t in range(1, shards)]
    pair = (near.astype(jnp.float32) + swap(far, group_bits[2]).astype(jnp.float32)).astype(jnp.bfloat16)
    other = swap(pair[rows:], group_bits[1])
    query_grad = pl.pallas_call(
        query_sum_kernel,
        out_shape=array((rows, width)),
        in_specs=[vmem] * 2,
        out_specs=vmem,
        compiler_params=small,
        cost_estimate=pl.CostEstimate(flops=1000000000, bytes_accessed=0, transcendentals=0),
        name="query_sum",
    )(pair, other)
    query_grad, *came = lax.optimization_barrier((query_grad, *came))
    key_grad, value_grad = pl.pallas_call(
        finish_kernel,
        out_shape=(array((part, hd)), array((part, hd))),
        in_specs=[vmem] * (len(came) + 1),
        out_specs=(vmem, vmem),
        compiler_params=small,
        name="finish",
    )(owned, *came)
    return query_grad, key_grad, value_grad


def solution(mesh):
    in_specs = (P("ctx", "head"), P("ctx", None), P("ctx", None), P("ctx", "head"), P(), P())
    out_specs = (P("ctx", "head"), P(("ctx", "head"), None), P(("ctx", "head"), None))
    return jax.shard_map(local, mesh=mesh, in_specs=in_specs, out_specs=out_specs, check_vma=False)
```

```python
import functools

import jax
import jax.numpy as jnp
from jax import lax
from jax.experimental import pallas as pl
from jax.experimental.pallas import tpu as pltpu
from jax.sharding import PartitionSpec as P

masked_value = -1e30
log2_e = 1.4426950408889634
GROUP = 4

NT = (((1,), (1,)), ((), ()))
NN = (((1,), (0,)), ((), ()))


def dot(a, b, dims):
    return lax.dot_general(a, b, dims, preferred_element_type=jnp.float32)


def offsets(size):
    group = (0, 1, 2, 3)
    return group, tuple(range(0, size, GROUP))


def place_kernel(group, chunk, docs, ints, place_ref):
    rows = place_ref.shape[1]
    count = (ints.shape[0] - docs) // 2
    index = lax.axis_index("ctx")
    half = rows // 2
    at = lax.broadcasted_iota(jnp.int32, (1, rows), 1)
    for j, bits in enumerate(group):
        first = ints[docs + (index ^ bits)] * half
        second = ints[docs + count + (index ^ bits)] * half - half
        pos = at + jnp.where(at < half, first, second)
        start = jnp.int32(0)
        opens = jnp.zeros_like(pos)
        for d in range(docs):
            opens = jnp.where(pos >= start, start, opens)
            start = start + ints[d]
        place_ref[j : j + 1, :] = pos
        place_ref[GROUP + j : GROUP + j + 1, :] = opens
    for b, bits in enumerate(chunk):
        for h in range(2):
            to = 2 * GROUP + 2 * b + h
            base = ints[docs + h * count + (index ^ bits)] * half
            place_ref[to : to + 1, :] = jnp.full((1, rows), base)


def both_heads(ref, heads, which):
    rows, hd = ref.shape[0] // 2, ref.shape[1] // heads
    at = pl.ds(which * rows, rows)
    return jnp.concatenate([ref[at, h * hd : (h + 1) * hd] for h in range(heads)], axis=0)


def stats_kernel(which, heads, place_ref, *refs):
    count = len(which)
    group, chunk = refs[:GROUP], refs[GROUP : GROUP + count]
    *before, out_ref, top_ref, expo_ref, dprobs_ref = refs[GROUP + count :]
    rows, width = chunk[0].shape
    hd = width // 2
    factor = hd ** (-0.5) * log2_e
    keys = jnp.concatenate([c[:, :hd] for c in chunk], axis=0)
    values = jnp.concatenate([c[:, hd:] for c in chunk], axis=0)
    at = lax.broadcasted_iota(jnp.int32, (rows // 2, rows), 0)
    spans = [2 * (GROUP + b) + h for b in which for h in range(2)]
    key_pos = jnp.concatenate([at + place_ref[s : s + 1, :] for s in spans], axis=0)
    for j in range(GROUP):
        pos, opens = place_ref[j : j + 1, :], place_ref[GROUP + j : GROUP + j + 1, :]
        allowed = (key_pos <= pos) & (key_pos >= opens)
        bias = jnp.where(allowed, 0.0, masked_value)
        bias = jnp.concatenate([bias] * heads, axis=1)
        scores = dot(keys, both_heads(group[j], heads, 0), NT) * factor + bias
        dprobs = dot(values, both_heads(group[j], heads, 1), NT)
        top = jnp.max(scores, axis=0, keepdims=True)
        expo = jnp.exp2(scores - top)
        total = jnp.sum(expo, axis=0, keepdims=True)
        log_total = top + jnp.log2(total)
        delta = jnp.sum(expo * dprobs, axis=0, keepdims=True) / total
        at_j = pl.ds(j * heads * rows, heads * rows)
        if before:
            parts = [jnp.concatenate([log_total, delta], axis=0), before[0][:, at_j]]
            log_total, delta = merged(parts)
        out_ref[0:1, at_j] = log_total
        out_ref[1:2, at_j] = delta
        top_ref[0:1, at_j] = top
        expo_ref[:, at_j] = expo
        dprobs_ref[:, at_j] = dprobs


def merged(parts):
    largest = functools.reduce(jnp.maximum, [p[0:1] for p in parts])
    share = [jnp.exp2(p[0:1] - largest) for p in parts]
    total = sum(share)
    delta = sum(w * p[1:2] for w, p in zip(share, parts)) / total
    return largest + jnp.log2(total), delta


def backward_kernel(order, late, heads, shards, *refs):
    chunks = len(order)
    group, chunk = refs[:GROUP], refs[GROUP : GROUP + chunks]
    chunk = chunk[late:] + chunk[:late]
    stats, refs = refs[GROUP + chunks :][:GROUP], refs[2 * GROUP + chunks :]
    (tops, expos, dprobs), refs = (refs[0:2], refs[2:4], refs[4:6]), refs[6:]
    near_ref, far_ref, *outs, dv_total, dk_total = refs
    rows, width = chunk[0].shape
    hd = width // 2
    shard = lax.axis_index("head")
    scaling = hd ** (-0.5)
    keys = jnp.concatenate([c[:, :hd] for c in chunk], axis=0)
    keys_across = keys.T
    for j in range(GROUP):
        at = pl.ds(j * heads * rows, heads * rows)
        parts = [
            s[0:2, pl.ds((j ^ t) * heads * rows, heads * rows)] for t, s in enumerate(stats)
        ]
        log_total, delta = merged(parts)
        weights = jnp.concatenate(
            [e[:, at] * jnp.exp2(t[0:1, at] - log_total) for e, t in zip(expos, tops)], axis=0
        )
        differences = jnp.concatenate([d[:, at] for d in dprobs], axis=0) - delta
        weights_low = weights.astype(jnp.bfloat16)
        dscores = (weights * differences).astype(jnp.bfloat16)
        dv = dot(weights_low, both_heads(group[j], heads, 1), NN)
        dk = dot(dscores, both_heads(group[j], heads, 0), NN)
        if j == 0:
            dv_total[...] = dv
            dk_total[...] = dk
        else:
            dv_total[...] += dv
            dk_total[...] += dk
        dq = ((dot(keys_across, dscores, NN) * scaling).T).astype(jnp.bfloat16)
        half = GROUP // 2
        to = (near_ref, far_ref)[j // half]
        for h in range(heads):
            to[pl.ds(j % half * rows, rows), h * hd : (h + 1) * hd] = dq[h * rows : (h + 1) * rows]
    part = rows // shards
    half = chunks // 2
    for t in range(shards):
        owner = lax.rem(shard + t, shards)
        for b in range(chunks):
            at = pl.ds(pl.multiple_of(order.index(b) * rows + owner * part, part), part)
            if b < half:
                out, to = outs[b], pl.ds(t * part, part)
            else:
                out, to = outs[half + t], pl.ds((b - half) * part, part)
            out[to, :hd] = (dk_total[at, :] * scaling).astype(jnp.bfloat16)
            out[to, hd:] = dv_total[at, :].astype(jnp.bfloat16)


def fold_kernel(*refs):
    total = refs[0][...].astype(jnp.float32)
    for ref in refs[1:-1]:
        total = total + ref[...].astype(jnp.float32)
    refs[-1][...] = total.astype(jnp.bfloat16)


def finish_kernel(owned_ref, *refs):
    *came, key_ref, value_ref = refs
    part, hd = key_ref.shape
    total = owned_ref[:part].astype(jnp.float32)
    for ref in came:
        total = total + ref[...].astype(jnp.float32)
    key_ref[...] = total[:, :hd].astype(jnp.bfloat16)
    value_ref[...] = total[:, hd:].astype(jnp.bfloat16)


def query_sum_kernel(pair_ref, other_ref, query_ref):
    rows = query_ref.shape[0]
    query = pair_ref[:rows].astype(jnp.float32) + other_ref[...].astype(jnp.float32)
    query_ref[...] = query.astype(jnp.bfloat16)


def local(queries, key_rows, value_rows, out_grad, doc_lengths, span_order):
    rows, width = queries.shape
    hd = key_rows.shape[1]
    heads = width // hd
    ctx_size, shards = lax.axis_size("ctx"), lax.axis_size("head")
    chunks = ctx_size // GROUP
    part = rows // shards
    group_bits, chunk_bits = offsets(ctx_size)

    def swap(x, bits):
        return lax.ppermute(x, "ctx", [(i, i ^ bits) for i in range(ctx_size)])

    def turn(x, by):
        return lax.ppermute(x, "head", [(i, (i + by) % shards) for i in range(shards)])

    vmem = pl.BlockSpec(memory_space=pltpu.VMEM)
    params = pltpu.CompilerParams(vmem_limit_bytes=40 * 1024 * 1024)
    small = pltpu.CompilerParams(vmem_limit_bytes=4 * 1024 * 1024)

    def array(shape, dtype=jnp.bfloat16):
        return jax.ShapeDtypeStruct(shape, dtype)

    place = pl.pallas_call(
        functools.partial(place_kernel, group_bits, chunk_bits, doc_lengths.shape[0]),
        out_shape=array((2 * (GROUP + chunks), rows), jnp.int32),
        in_specs=[pl.BlockSpec(memory_space=pltpu.SMEM)],
        out_specs=vmem,
        compiler_params=small,
        cost_estimate=pl.CostEstimate(flops=1000000000, bytes_accessed=0, transcendentals=0),
        name="place",
    )(jnp.concatenate([doc_lengths, span_order.T.reshape(-1)]))

    packed = jnp.concatenate(
        [jnp.concatenate([key_rows, value_rows], axis=1), queries, out_grad], axis=0
    )
    packed = lax.optimization_barrier(packed)
    packed_kv, packed_qg = packed[:rows], packed[rows:]
    chunk = [packed_kv] + [swap(packed_kv, bits) for bits in chunk_bits[1:]]
    across = swap(packed_qg, group_bits[2])
    beside = swap(packed_qg, group_bits[1])
    group = [packed_qg, beside, across, swap(across, group_bits[1])]

    late = tuple(range(1, 3 * chunks // 4))
    early = (0, *range(3 * chunks // 4, chunks))

    def stats_of(which, before, flops):
        wide = array((len(which) * rows, GROUP * heads * rows), jnp.float32)
        return pl.pallas_call(
            functools.partial(stats_kernel, which, heads),
            out_shape=(
                array((2, GROUP * heads * rows), jnp.float32),
                array((1, GROUP * heads * rows), jnp.float32),
                wide,
                wide,
            ),
            in_specs=[vmem] * (1 + GROUP + len(which) + len(before)),
            out_specs=(vmem, vmem, vmem, vmem),
            compiler_params=params,
            cost_estimate=pl.CostEstimate(flops=flops, bytes_accessed=0, transcendentals=0),
            name="stats",
        )(place, *group, *[chunk[b] for b in which], *before)

    first, *kept_early = stats_of(early, (), 0)
    stats, *kept_late = stats_of(late, (first,), 0)
    kept = [ref for pair in zip(kept_early, kept_late) for ref in pair]
    all_stats = [stats] + [swap(stats, bits) for bits in group_bits[1:]]

    pair_rows = array((GROUP // 2 * rows, width))
    half = chunks // 2
    pieces = (array((rows, 2 * hd)),) * half + (array((half * part, 2 * hd)),) * shards
    near, far, *dkv = pl.pallas_call(
        functools.partial(backward_kernel, early + late, len(late), heads, shards),
        out_shape=(pair_rows, pair_rows) + pieces,
        in_specs=[vmem] * (2 * GROUP + chunks + len(kept)),
        out_specs=(vmem,) * (2 + len(pieces)),
        scratch_shapes=[pltpu.VMEM((chunks * rows, hd), jnp.float32)] * 2,
        compiler_params=params,
        name="backward",
    )(*group, *[chunk[b] for b in late + early], *all_stats, *kept)

    def fold(parts, flops):
        return pl.pallas_call(
            fold_kernel,
            out_shape=jax.ShapeDtypeStruct(parts[0].shape, jnp.bfloat16),
            in_specs=[vmem] * len(parts),
            out_specs=vmem,
            compiler_params=small,
            cost_estimate=pl.CostEstimate(flops=flops, bytes_accessed=0, transcendentals=0),
            name="fold",
        )(*parts)

    across = fold([dkv[half]] + [turn(dkv[half + t], t) for t in range(1, shards)], 0)
    owned = fold([dkv[0]] + [swap(dkv[b], chunk_bits[b]) for b in range(1, half)], 1000000000)
    came = [
        swap(across[k * part : (k + 1) * part], chunk_bits[half + k]) for k in range(half)[::-1]
    ] + [turn(owned[t * part : (t + 1) * part], t) for t in range(1, shards)]
    pair = (near.astype(jnp.float32) + swap(far, group_bits[2]).astype(jnp.float32)).astype(jnp.bfloat16)
    other = swap(pair[rows:], group_bits[1])
    query_grad = pl.pallas_call(
        query_sum_kernel,
        out_shape=array((rows, width)),
        in_specs=[vmem] * 2,
        out_specs=vmem,
        compiler_params=small,
        cost_estimate=pl.CostEstimate(flops=1000000000, bytes_accessed=0, transcendentals=0),
        name="query_sum",
    )(pair, other)
    query_grad, *came = lax.optimization_barrier((query_grad, *came))
    key_grad, value_grad = pl.pallas_call(
        finish_kernel,
        out_shape=(array((part, hd)), array((part, hd))),
        in_specs=[vmem] * (len(came) + 1),
        out_specs=(vmem, vmem),
        compiler_params=small,
        name="finish",
    )(owned, *came)
    return query_grad, key_grad, value_grad


def solution(mesh):
    in_specs = (P("ctx", "head"), P("ctx", None), P("ctx", None), P("ctx", "head"), P(), P())
    out_specs = (P("ctx", "head"), P(("ctx", "head"), None), P(("ctx", "head"), None))
    return jax.shard_map(local, mesh=mesh, in_specs=in_specs, out_specs=out_specs, check_vma=False)
```

```python
import functools

import jax
import jax.numpy as jnp
from jax import lax
from jax.experimental import pallas as pl
from jax.experimental.pallas import tpu as pltpu
from jax.sharding import PartitionSpec as P

masked_value = -1e30
log2_e = 1.4426950408889634
GROUP = 4

NT = (((1,), (1,)), ((), ()))
NN = (((1,), (0,)), ((), ()))


def dot(a, b, dims):
    return lax.dot_general(a, b, dims, preferred_element_type=jnp.float32)


def offsets(size):
    group = (0, 1, 2, 3)
    return group, tuple(range(0, size, GROUP))


def place_kernel(group, chunk, docs, ints, place_ref):
    rows = place_ref.shape[1]
    count = (ints.shape[0] - docs) // 2
    index = lax.axis_index("ctx")
    half = rows // 2
    at = lax.broadcasted_iota(jnp.int32, (1, rows), 1)
    for j, bits in enumerate(group):
        first = ints[docs + (index ^ bits)] * half
        second = ints[docs + count + (index ^ bits)] * half - half
        pos = at + jnp.where(at < half, first, second)
        start = jnp.int32(0)
        opens = jnp.zeros_like(pos)
        for d in range(docs):
            opens = jnp.where(pos >= start, start, opens)
            start = start + ints[d]
        place_ref[j : j + 1, :] = pos
        place_ref[GROUP + j : GROUP + j + 1, :] = opens
    for b, bits in enumerate(chunk):
        for h in range(2):
            to = 2 * GROUP + 2 * b + h
            base = ints[docs + h * count + (index ^ bits)] * half
            place_ref[to : to + 1, :] = jnp.full((1, rows), base)


def both_heads(ref, heads, which):
    rows, hd = ref.shape[0] // 2, ref.shape[1] // heads
    at = pl.ds(which * rows, rows)
    return jnp.concatenate([ref[at, h * hd : (h + 1) * hd] for h in range(heads)], axis=0)


def stats_kernel(which, heads, place_ref, *refs):
    count = len(which)
    group, chunk = refs[:GROUP], refs[GROUP : GROUP + count]
    *before, out_ref, top_ref, expo_ref, dprobs_ref = refs[GROUP + count :]
    rows, width = chunk[0].shape
    hd = width // 2
    factor = hd ** (-0.5) * log2_e
    keys = jnp.concatenate([c[:, :hd] for c in chunk], axis=0)
    values = jnp.concatenate([c[:, hd:] for c in chunk], axis=0)
    at = lax.broadcasted_iota(jnp.int32, (rows // 2, rows), 0)
    spans = [2 * (GROUP + b) + h for b in which for h in range(2)]
    key_pos = jnp.concatenate([at + place_ref[s : s + 1, :] for s in spans], axis=0)
    for j in range(GROUP):
        pos, opens = place_ref[j : j + 1, :], place_ref[GROUP + j : GROUP + j + 1, :]
        allowed = (key_pos <= pos) & (key_pos >= opens)
        bias = jnp.where(allowed, 0.0, masked_value)
        bias = jnp.concatenate([bias] * heads, axis=1)
        scores = dot(keys, both_heads(group[j], heads, 0), NT) * factor + bias
        dprobs = dot(values, both_heads(group[j], heads, 1), NT)
        top = jnp.max(scores, axis=0, keepdims=True)
        expo = jnp.exp2(scores - top)
        total = jnp.sum(expo, axis=0, keepdims=True)
        log_total = top + jnp.log2(total)
        delta = jnp.sum(expo * dprobs, axis=0, keepdims=True) / total
        at_j = pl.ds(j * heads * rows, heads * rows)
        if before:
            parts = [jnp.concatenate([log_total, delta], axis=0), before[0][:, at_j]]
            log_total, delta = merged(parts)
        out_ref[0:1, at_j] = log_total
        out_ref[1:2, at_j] = delta
        top_ref[0:1, at_j] = top
        expo_ref[:, at_j] = expo
        dprobs_ref[:, at_j] = dprobs


def merged(parts):
    largest = functools.reduce(jnp.maximum, [p[0:1] for p in parts])
    share = [jnp.exp2(p[0:1] - largest) for p in parts]
    total = sum(share)
    delta = sum(w * p[1:2] for w, p in zip(share, parts)) / total
    return largest + jnp.log2(total), delta


def backward_kernel(some, kept_at, heads, shards, whole, *refs):
    group, stats, refs = refs[:GROUP], refs[GROUP : 2 * GROUP], refs[2 * GROUP :]
    tops, expos, dprobs, refs = refs[0:2], refs[2:4], refs[4:6], refs[6:]
    rows, hd = group[0].shape[0] // 2, group[0].shape[1] // heads
    if whole:
        chunk, (other_ref, near_ref, far_ref, *outs, dv_total, dk_total) = (
            refs[: len(kept_at)],
            refs[len(kept_at) :],
        )
        keys_across = jnp.concatenate([c[:, :hd] for c in chunk], axis=0).T
    else:
        dscores_ref, *outs, dv_total, dk_total = refs
    shard = lax.axis_index("head")
    scaling = hd ** (-0.5)
    pair = GROUP // 2
    for j in range(GROUP):
        at = pl.ds(j * heads * rows, heads * rows)
        parts = [
            s[0:2, pl.ds((j ^ t) * heads * rows, heads * rows)] for t, s in enumerate(stats)
        ]
        log_total, delta = merged(parts)
        factor = [jnp.exp2(t[0:1, at] - log_total) for t in tops]
        weights, dscores = [], []
        for b in some:
            part, first = kept_at[b]
            kept = pl.ds(first * rows, rows)
            weights.append(expos[part][kept, at] * factor[part])
            dscores.append(weights[-1] * (dprobs[part][kept, at] - delta))
        weights = jnp.concatenate(weights, axis=0).astype(jnp.bfloat16)
        dscores = jnp.concatenate(dscores, axis=0).astype(jnp.bfloat16)
        dv = dot(weights, both_heads(group[j], heads, 1), NN)
        dk = dot(dscores, both_heads(group[j], heads, 0), NN)
        if j == 0:
            dv_total[...] = dv
            dk_total[...] = dk
        else:
            dv_total[...] += dv
            dk_total[...] += dk
        if not whole:
            dscores_ref[:, at] = dscores
            continue
        dscores = jnp.concatenate([dscores, other_ref[:, at]], axis=0)
        dq = ((dot(keys_across, dscores, NN) * scaling).T).astype(jnp.bfloat16)
        to = (near_ref, far_ref)[j // pair]
        for h in range(heads):
            to[pl.ds(j % pair * rows, rows), h * hd : (h + 1) * hd] = dq[h * rows : (h + 1) * rows]
    size = rows // shards
    for t in range(shards):
        owner = lax.rem(shard + t, shards)
        for k in range(len(some)):
            at = pl.ds(pl.multiple_of(k * rows + owner * size, size), size)
            out, to = outs[t], pl.ds(k * size, size)
            out[to, :hd] = (dk_total[at, :] * scaling).astype(jnp.bfloat16)
            out[to, hd:] = dv_total[at, :].astype(jnp.bfloat16)


def fold_kernel(*refs):
    total = refs[0][...].astype(jnp.float32)
    for ref in refs[1:-1]:
        total = total + ref[...].astype(jnp.float32)
    refs[-1][...] = total.astype(jnp.bfloat16)


def finish_kernel(owned_ref, *refs):
    *came, key_ref, value_ref = refs
    part, hd = key_ref.shape
    total = owned_ref[:part].astype(jnp.float32)
    for ref in came:
        total = total + ref[...].astype(jnp.float32)
    key_ref[...] = total[:, :hd].astype(jnp.bfloat16)
    value_ref[...] = total[:, hd:].astype(jnp.bfloat16)


def query_sum_kernel(pair_ref, other_ref, query_ref):
    rows = query_ref.shape[0]
    query = pair_ref[:rows].astype(jnp.float32) + other_ref[...].astype(jnp.float32)
    query_ref[...] = query.astype(jnp.bfloat16)


def local(queries, key_rows, value_rows, out_grad, doc_lengths, span_order):
    rows, width = queries.shape
    hd = key_rows.shape[1]
    heads = width // hd
    ctx_size, shards = lax.axis_size("ctx"), lax.axis_size("head")
    chunks = ctx_size // GROUP
    part = rows // shards
    group_bits, chunk_bits = offsets(ctx_size)

    def swap(x, bits):
        return lax.ppermute(x, "ctx", [(i, i ^ bits) for i in range(ctx_size)])

    def turn(x, by):
        return lax.ppermute(x, "head", [(i, (i + by) % shards) for i in range(shards)])

    vmem = pl.BlockSpec(memory_space=pltpu.VMEM)
    params = pltpu.CompilerParams(vmem_limit_bytes=40 * 1024 * 1024)
    small = pltpu.CompilerParams(vmem_limit_bytes=4 * 1024 * 1024)

    order = pl.CostEstimate(flops=0, bytes_accessed=0, transcendentals=0)

    def array(shape, dtype=jnp.bfloat16):
        return jax.ShapeDtypeStruct(shape, dtype)

    place = pl.pallas_call(
        functools.partial(place_kernel, group_bits, chunk_bits, doc_lengths.shape[0]),
        out_shape=array((2 * (GROUP + chunks), rows), jnp.int32),
        in_specs=[pl.BlockSpec(memory_space=pltpu.SMEM)],
        out_specs=vmem,
        compiler_params=small,
        cost_estimate=pl.CostEstimate(flops=10000000000, bytes_accessed=0, transcendentals=0),
        name="place",
    )(jnp.concatenate([doc_lengths, span_order.T.reshape(-1)]))

    packed = jnp.concatenate(
        [jnp.concatenate([key_rows, value_rows], axis=1), queries, out_grad], axis=0
    )
    packed = lax.optimization_barrier(packed)
    packed_kv, packed_qg = packed[:rows], packed[rows:]
    chunk = [packed_kv] + [swap(packed_kv, bits) for bits in chunk_bits[1:]]
    across = swap(packed_qg, group_bits[2])
    both = swap(jnp.concatenate([packed_qg, across], axis=0), group_bits[1])
    group = [packed_qg, both[: 2 * rows], across, both[2 * rows :]]

    late = tuple(range(1, 3 * chunks // 4))[::-1]
    early = (0, *range(3 * chunks // 4, chunks))

    def stats_of(which, before):
        wide = array((len(which) * rows, GROUP * heads * rows), jnp.float32)
        return pl.pallas_call(
            functools.partial(stats_kernel, which, heads),
            out_shape=(
                array((2, GROUP * heads * rows), jnp.float32),
                array((1, GROUP * heads * rows), jnp.float32),
                wide,
                wide,
            ),
            in_specs=[vmem] * (1 + GROUP + len(which) + len(before)),
            out_specs=(vmem, vmem, vmem, vmem),
            compiler_params=params,
            cost_estimate=order,
            name="stats",
        )(place, *group, *[chunk[b] for b in which], *before)

    first, *kept_early = stats_of(early, ())
    stats, *kept_late = stats_of(late, (first,))
    kept = [ref for both in zip(kept_early, kept_late) for ref in both]
    kept_at = [(0, early.index(b)) if b in early else (1, late.index(b)) for b in range(chunks)]
    all_stats = [stats] + [swap(stats, bits) for bits in group_bits[1:]]

    half = chunks // 2
    near_chunks, far_chunks = tuple(range(half)), tuple(range(half, chunks))

    def backward_of(some, given, out_shape):
        return pl.pallas_call(
            functools.partial(backward_kernel, some, kept_at, heads, shards, len(given) > 0),
            out_shape=out_shape,
            in_specs=[vmem] * (2 * GROUP + len(kept) + len(given)),
            out_specs=(vmem,) * len(out_shape),
            scratch_shapes=[pltpu.VMEM((len(some) * rows, hd), jnp.float32)] * 2,
            compiler_params=params,
            cost_estimate=order,
            name="backward",
        )(*group, *all_stats, *kept, *given)

    pair_rows = array((GROUP // 2 * rows, width))
    piece = (array((half * part, 2 * hd)),) * shards
    dscores, *dkv_far = backward_of(
        far_chunks, (), (array((half * rows, GROUP * heads * rows)),) + piece
    )
    near, far, *dkv_near = backward_of(
        near_chunks,
        (*[chunk[b] for b in near_chunks + far_chunks], dscores),
        (pair_rows, pair_rows) + piece,
    )

    def fold(parts, flops=0):
        return pl.pallas_call(
            fold_kernel,
            out_shape=jax.ShapeDtypeStruct(parts[0].shape, jnp.bfloat16),
            in_specs=[vmem] * len(parts),
            out_specs=vmem,
            compiler_params=small,
            cost_estimate=pl.CostEstimate(flops=flops, bytes_accessed=0, transcendentals=0),
            name="fold",
        )(*parts)

    far_sum = fold([dkv_far[0]] + [turn(dkv_far[t], t) for t in range(1, shards)])
    near_sum = fold([dkv_near[0]] + [turn(dkv_near[t], t) for t in range(1, shards)], 1000000000)
    sums = (near_sum, far_sum)

    def arrived(b):
        return swap(sums[b // half][b % half * part :][:part], chunk_bits[b])

    owned = near_sum
    came = [arrived(b) for b in (*range(1, half), *range(half, chunks)[::-1])]
    pair = near.astype(jnp.float32) + swap(far, group_bits[2]).astype(jnp.float32)
    pair = pair.astype(jnp.bfloat16)
    other = swap(pair[rows:], group_bits[1])
    query_grad = pl.pallas_call(
        query_sum_kernel,
        out_shape=array((rows, width)),
        in_specs=[vmem] * 2,
        out_specs=vmem,
        compiler_params=small,
        cost_estimate=pl.CostEstimate(flops=1000000000, bytes_accessed=0, transcendentals=0),
        name="query_sum",
    )(pair, other)
    query_grad, *came = lax.optimization_barrier((query_grad, *came))
    key_grad, value_grad = pl.pallas_call(
        finish_kernel,
        out_shape=(array((part, hd)), array((part, hd))),
        in_specs=[vmem] * (len(came) + 1),
        out_specs=(vmem, vmem),
        compiler_params=small,
        name="finish",
    )(owned, *came)
    return query_grad, key_grad, value_grad


def solution(mesh):
    in_specs = (P("ctx", "head"), P("ctx", None), P("ctx", None), P("ctx", "head"), P(), P())
    out_specs = (P("ctx", "head"), P(("ctx", "head"), None), P(("ctx", "head"), None))
    return jax.shard_map(local, mesh=mesh, in_specs=in_specs, out_specs=out_specs, check_vma=False)
```

```python
import functools

import jax
import jax.numpy as jnp
from jax import lax
from jax.experimental import pallas as pl
from jax.experimental.pallas import tpu as pltpu
from jax.sharding import PartitionSpec as P

masked_value = -1e30
log2_e = 1.4426950408889634
GROUP = 4

NT = (((1,), (1,)), ((), ()))
NN = (((1,), (0,)), ((), ()))


def dot(a, b, dims):
    return lax.dot_general(a, b, dims, preferred_element_type=jnp.float32)


def offsets(size):
    group = (0, 1, 2, 3)
    return group, tuple(range(0, size, GROUP))


def place_kernel(group, chunk, docs, ints, place_ref):
    rows = place_ref.shape[1]
    count = (ints.shape[0] - docs) // 2
    index = lax.axis_index("ctx")
    half = rows // 2
    at = lax.broadcasted_iota(jnp.int32, (1, rows), 1)
    for j, bits in enumerate(group):
        first = ints[docs + (index ^ bits)] * half
        second = ints[docs + count + (index ^ bits)] * half - half
        pos = at + jnp.where(at < half, first, second)
        start = jnp.int32(0)
        opens = jnp.zeros_like(pos)
        for d in range(docs):
            opens = jnp.where(pos >= start, start, opens)
            start = start + ints[d]
        place_ref[j : j + 1, :] = pos
        place_ref[GROUP + j : GROUP + j + 1, :] = opens
    for b, bits in enumerate(chunk):
        for h in range(2):
            to = 2 * GROUP + 2 * b + h
            origin = lax.rem(index + bits, count)
            base = ints[docs + h * count + origin] * half
            place_ref[to : to + 1, :] = jnp.full((1, rows), base)


def both_heads(ref, heads, which):
    rows, hd = ref.shape[0] // 2, ref.shape[1] // heads
    at = pl.ds(which * rows, rows)
    return jnp.concatenate([ref[at, h * hd : (h + 1) * hd] for h in range(heads)], axis=0)


def stats_kernel(which, heads, place_ref, *refs):
    count = len(which)
    group, chunk = refs[:GROUP], refs[GROUP : GROUP + count]
    *before, out_ref, top_ref, expo_ref, dprobs_ref = refs[GROUP + count :]
    rows, width = chunk[0].shape
    hd = width // 2
    factor = hd ** (-0.5) * log2_e
    keys = jnp.concatenate([c[:, :hd] for c in chunk], axis=0)
    values = jnp.concatenate([c[:, hd:] for c in chunk], axis=0)
    at = lax.broadcasted_iota(jnp.int32, (rows // 2, rows), 0)
    spans = [2 * (GROUP + b) + h for b in which for h in range(2)]
    key_pos = jnp.concatenate([at + place_ref[s : s + 1, :] for s in spans], axis=0)
    for j in range(GROUP):
        pos, opens = place_ref[j : j + 1, :], place_ref[GROUP + j : GROUP + j + 1, :]
        allowed = (key_pos <= pos) & (key_pos >= opens)
        bias = jnp.where(allowed, 0.0, masked_value)
        bias = jnp.concatenate([bias] * heads, axis=1)
        scores = dot(keys, both_heads(group[j], heads, 0), NT) * factor + bias
        dprobs = dot(values, both_heads(group[j], heads, 1), NT)
        top = jnp.max(scores, axis=0, keepdims=True)
        expo = jnp.exp2(scores - top)
        total = jnp.sum(expo, axis=0, keepdims=True)
        log_total = top + jnp.log2(total)
        delta = jnp.sum(expo * dprobs, axis=0, keepdims=True) / total
        at_j = pl.ds(j * heads * rows, heads * rows)
        if before:
            parts = [jnp.concatenate([log_total, delta], axis=0), before[0][:, at_j]]
            log_total, delta = merged(parts)
        out_ref[0:1, at_j] = log_total
        out_ref[1:2, at_j] = delta
        top_ref[0:1, at_j] = top
        expo_ref[:, at_j] = expo
        dprobs_ref[:, at_j] = dprobs


def merged(parts):
    largest = functools.reduce(jnp.maximum, [p[0:1] for p in parts])
    share = [jnp.exp2(p[0:1] - largest) for p in parts]
    total = sum(share)
    delta = sum(w * p[1:2] for w, p in zip(share, parts)) / total
    return largest + jnp.log2(total), delta


def backward_kernel(order, late, heads, shards, *refs):
    chunks = len(order)
    group, chunk = refs[:GROUP], refs[GROUP : GROUP + chunks]
    chunk = chunk[late:] + chunk[:late]
    stats, refs = refs[GROUP + chunks :][:GROUP], refs[2 * GROUP + chunks :]
    (tops, expos, dprobs), refs = (refs[0:2], refs[2:4], refs[4:6]), refs[6:]
    near_ref, far_ref, *outs, dv_total, dk_total = refs
    rows, width = chunk[0].shape
    hd = width // 2
    shard = lax.axis_index("head")
    plane = lax.axis_index("ctx") // GROUP
    scaling = hd ** (-0.5)
    keys = jnp.concatenate([c[:, :hd] for c in chunk], axis=0)
    keys_across = keys.T
    for j in range(GROUP):
        at = pl.ds(j * heads * rows, heads * rows)
        parts = [
            s[0:2, pl.ds((j ^ t) * heads * rows, heads * rows)] for t, s in enumerate(stats)
        ]
        log_total, delta = merged(parts)
        weights = jnp.concatenate(
            [e[:, at] * jnp.exp2(t[0:1, at] - log_total) for e, t in zip(expos, tops)], axis=0
        )
        differences = jnp.concatenate([d[:, at] for d in dprobs], axis=0) - delta
        weights_low = weights.astype(jnp.bfloat16)
        dscores = (weights * differences).astype(jnp.bfloat16)
        dv = dot(weights_low, both_heads(group[j], heads, 1), NN)
        dk = dot(dscores, both_heads(group[j], heads, 0), NN)
        if j == 0:
            dv_total[...] = dv
            dk_total[...] = dk
        else:
            dv_total[...] += dv
            dk_total[...] += dk
        dq = ((dot(keys_across, dscores, NN) * scaling).T).astype(jnp.bfloat16)
        half = GROUP // 2
        to = (near_ref, far_ref)[j // half]
        for h in range(heads):
            to[pl.ds(j % half * rows, rows), h * hd : (h + 1) * hd] = dq[h * rows : (h + 1) * rows]
    part = rows // shards
    half = chunks // 2
    for t in range(shards):
        owner = lax.rem(shard + t, shards)
        for b in range(chunks):
            came = lax.rem((plane ^ b) - plane + chunks, chunks)
            at = sum(jnp.where(came == k, order.index(k), 0) for k in range(chunks))
            at = pl.ds(pl.multiple_of(at * rows + owner * part, part), part)
            if b < half:
                out, to = outs[b], pl.ds(t * part, part)
            else:
                out, to = outs[half + t], pl.ds((b - half) * part, part)
            out[to, :hd] = (dk_total[at, :] * scaling).astype(jnp.bfloat16)
            out[to, hd:] = dv_total[at, :].astype(jnp.bfloat16)


def fold_kernel(*refs):
    total = refs[0][...].astype(jnp.float32)
    for ref in refs[1:-1]:
        total = total + ref[...].astype(jnp.float32)
    refs[-1][...] = total.astype(jnp.bfloat16)


def finish_kernel(owned_ref, *refs):
    *came, key_ref, value_ref = refs
    part, hd = key_ref.shape
    total = owned_ref[:part].astype(jnp.float32)
    for ref in came:
        total = total + ref[...].astype(jnp.float32)
    key_ref[...] = total[:, :hd].astype(jnp.bfloat16)
    value_ref[...] = total[:, hd:].astype(jnp.bfloat16)


def query_sum_kernel(pair_ref, other_ref, query_ref):
    rows = query_ref.shape[0]
    query = pair_ref[:rows].astype(jnp.float32) + other_ref[...].astype(jnp.float32)
    query_ref[...] = query.astype(jnp.bfloat16)


def local(queries, key_rows, value_rows, out_grad, doc_lengths, span_order):
    rows, width = queries.shape
    hd = key_rows.shape[1]
    heads = width // hd
    ctx_size, shards = lax.axis_size("ctx"), lax.axis_size("head")
    chunks = ctx_size // GROUP
    part = rows // shards
    group_bits, chunk_bits = offsets(ctx_size)

    def swap(x, bits):
        return lax.ppermute(x, "ctx", [(i, i ^ bits) for i in range(ctx_size)])

    def shift(x, by):
        return lax.ppermute(x, "ctx", [(i, (i - by) % ctx_size) for i in range(ctx_size)])

    def turn(x, by):
        return lax.ppermute(x, "head", [(i, (i + by) % shards) for i in range(shards)])

    vmem = pl.BlockSpec(memory_space=pltpu.VMEM)
    params = pltpu.CompilerParams(vmem_limit_bytes=40 * 1024 * 1024)
    small = pltpu.CompilerParams(vmem_limit_bytes=4 * 1024 * 1024)

    def array(shape, dtype=jnp.bfloat16):
        return jax.ShapeDtypeStruct(shape, dtype)

    place = pl.pallas_call(
        functools.partial(place_kernel, group_bits, chunk_bits, doc_lengths.shape[0]),
        out_shape=array((2 * (GROUP + chunks), rows), jnp.int32),
        in_specs=[pl.BlockSpec(memory_space=pltpu.SMEM)],
        out_specs=vmem,
        compiler_params=small,
        cost_estimate=pl.CostEstimate(flops=10000000000, bytes_accessed=0, transcendentals=0),
        name="place",
    )(jnp.concatenate([doc_lengths, span_order.T.reshape(-1)]))

    packed = jnp.concatenate(
        [jnp.concatenate([key_rows, value_rows], axis=1), queries, out_grad], axis=0
    )
    packed = lax.optimization_barrier(packed)
    packed_kv, packed_qg = packed[:rows], packed[rows:]
    chunk = [packed_kv] + [shift(packed_kv, bits) for bits in chunk_bits[1:]]
    across = swap(packed_qg, group_bits[2])
    both = swap(jnp.concatenate([packed_qg, across], axis=0), group_bits[1])
    group = [packed_qg, both[: 2 * rows], across, both[2 * rows :]]

    late = tuple(range(1, 3 * chunks // 4))
    early = (0, *range(3 * chunks // 4, chunks))

    def stats_of(which, before, flops):
        wide = array((len(which) * rows, GROUP * heads * rows), jnp.float32)
        return pl.pallas_call(
            functools.partial(stats_kernel, which, heads),
            out_shape=(
                array((2, GROUP * heads * rows), jnp.float32),
                array((1, GROUP * heads * rows), jnp.float32),
                wide,
                wide,
            ),
            in_specs=[vmem] * (1 + GROUP + len(which) + len(before)),
            out_specs=(vmem, vmem, vmem, vmem),
            compiler_params=params,
            cost_estimate=pl.CostEstimate(flops=flops, bytes_accessed=0, transcendentals=0),
            name="stats",
        )(place, *group, *[chunk[b] for b in which], *before)

    first, *kept_early = stats_of(early, (), 0)
    stats, *kept_late = stats_of(late, (first,), 0)
    kept = [ref for pair in zip(kept_early, kept_late) for ref in pair]
    all_stats = [stats] + [swap(stats, bits) for bits in group_bits[1:]]

    pair_rows = array((GROUP // 2 * rows, width))
    half = chunks // 2
    pieces = (array((rows, 2 * hd)),) * half + (array((half * part, 2 * hd)),) * shards
    near, far, *dkv = pl.pallas_call(
        functools.partial(backward_kernel, early + late, len(late), heads, shards),
        out_shape=(pair_rows, pair_rows) + pieces,
        in_specs=[vmem] * (2 * GROUP + chunks + len(kept)),
        out_specs=(vmem,) * (2 + len(pieces)),
        scratch_shapes=[pltpu.VMEM((chunks * rows, hd), jnp.float32)] * 2,
        compiler_params=params,
        name="backward",
    )(*group, *[chunk[b] for b in late + early], *all_stats, *kept)

    def fold(parts, flops):
        return pl.pallas_call(
            fold_kernel,
            out_shape=jax.ShapeDtypeStruct(parts[0].shape, jnp.bfloat16),
            in_specs=[vmem] * len(parts),
            out_specs=vmem,
            compiler_params=small,
            cost_estimate=pl.CostEstimate(flops=flops, bytes_accessed=0, transcendentals=0),
            name="fold",
        )(*parts)

    across = fold([dkv[half]] + [turn(dkv[half + t], t) for t in range(1, shards)], 0)
    owned = fold([dkv[0]] + [swap(dkv[b], chunk_bits[b]) for b in range(1, half)], 1000000000)
    came = [
        swap(across[k * part : (k + 1) * part], chunk_bits[half + k]) for k in range(half)
    ] + [turn(owned[t * part : (t + 1) * part], t) for t in range(1, shards)]
    pair = (near.astype(jnp.float32) + swap(far, group_bits[2]).astype(jnp.float32)).astype(jnp.bfloat16)
    other = swap(pair[rows:], group_bits[1])
    query_grad = pl.pallas_call(
        query_sum_kernel,
        out_shape=array((rows, width)),
        in_specs=[vmem] * 2,
        out_specs=vmem,
        compiler_params=small,
        cost_estimate=pl.CostEstimate(flops=1000000000, bytes_accessed=0, transcendentals=0),
        name="query_sum",
    )(pair, other)
    query_grad, *came = lax.optimization_barrier((query_grad, *came))
    key_grad, value_grad = pl.pallas_call(
        finish_kernel,
        out_shape=(array((part, hd)), array((part, hd))),
        in_specs=[vmem] * (len(came) + 1),
        out_specs=(vmem, vmem),
        compiler_params=small,
        name="finish",
    )(owned, *came)
    return query_grad, key_grad, value_grad


def solution(mesh):
    in_specs = (P("ctx", "head"), P("ctx", None), P("ctx", None), P("ctx", "head"), P(), P())
    out_specs = (P("ctx", "head"), P(("ctx", "head"), None), P(("ctx", "head"), None))
    return jax.shard_map(local, mesh=mesh, in_specs=in_specs, out_specs=out_specs, check_vma=False)
```

```python
import functools

import jax
import jax.numpy as jnp
from jax import lax
from jax.experimental import pallas as pl
from jax.experimental.pallas import tpu as pltpu
from jax.sharding import PartitionSpec as P

masked_value = -1e30
log2_e = 1.4426950408889634
GROUP = 4

NT = (((1,), (1,)), ((), ()))
NN = (((1,), (0,)), ((), ()))


def dot(a, b, dims):
    return lax.dot_general(a, b, dims, preferred_element_type=jnp.float32)


def offsets(size):
    group = (0, 1, 2, 3)
    return group, tuple(range(0, size, GROUP))


def place_kernel(group, chunk, docs, ints, place_ref):
    rows = place_ref.shape[1]
    count = (ints.shape[0] - docs) // 2
    index = lax.axis_index("ctx")
    half = rows // 2
    at = lax.broadcasted_iota(jnp.int32, (1, rows), 1)
    for j, bits in enumerate(group):
        first = ints[docs + (index ^ bits)] * half
        second = ints[docs + count + (index ^ bits)] * half - half
        pos = at + jnp.where(at < half, first, second)
        start = jnp.int32(0)
        opens = jnp.zeros_like(pos)
        for d in range(docs):
            opens = jnp.where(pos >= start, start, opens)
            start = start + ints[d]
        place_ref[j : j + 1, :] = pos
        place_ref[GROUP + j : GROUP + j + 1, :] = opens
    for b, bits in enumerate(chunk):
        for h in range(2):
            to = 2 * GROUP + 2 * b + h
            origin = lax.rem(index + bits, count)
            base = ints[docs + h * count + origin] * half
            place_ref[to : to + 1, :] = jnp.full((1, rows), base)


def both_heads(ref, heads, which):
    rows, hd = ref.shape[0] // 2, ref.shape[1] // heads
    at = pl.ds(which * rows, rows)
    return jnp.concatenate([ref[at, h * hd : (h + 1) * hd] for h in range(heads)], axis=0)


def stats_kernel(which, heads, place_ref, *refs):
    count = len(which)
    group, chunk = refs[:GROUP], refs[GROUP : GROUP + count]
    *before, out_ref, top_ref, expo_ref, dprobs_ref = refs[GROUP + count :]
    rows, width = chunk[0].shape
    hd = width // 2
    factor = hd ** (-0.5) * log2_e
    keys = jnp.concatenate([c[:, :hd] for c in chunk], axis=0)
    values = jnp.concatenate([c[:, hd:] for c in chunk], axis=0)
    at = lax.broadcasted_iota(jnp.int32, (rows // 2, rows), 0)
    spans = [2 * (GROUP + b) + h for b in which for h in range(2)]
    key_pos = jnp.concatenate([at + place_ref[s : s + 1, :] for s in spans], axis=0)
    for j in range(GROUP):
        pos, opens = place_ref[j : j + 1, :], place_ref[GROUP + j : GROUP + j + 1, :]
        allowed = (key_pos <= pos) & (key_pos >= opens)
        bias = jnp.where(allowed, 0.0, masked_value)
        bias = jnp.concatenate([bias] * heads, axis=1)
        scores = dot(keys, both_heads(group[j], heads, 0), NT) * factor + bias
        dprobs = dot(values, both_heads(group[j], heads, 1), NT)
        top = jnp.max(scores, axis=0, keepdims=True)
        expo = jnp.exp2(scores - top)
        total = jnp.sum(expo, axis=0, keepdims=True)
        log_total = top + jnp.log2(total)
        delta = jnp.sum(expo * dprobs, axis=0, keepdims=True) / total
        at_j = pl.ds(j * heads * rows, heads * rows)
        if before:
            parts = [jnp.concatenate([log_total, delta], axis=0), before[0][:, at_j]]
            log_total, delta = merged(parts)
        out_ref[0:1, at_j] = log_total
        out_ref[1:2, at_j] = delta
        top_ref[0:1, at_j] = top
        expo_ref[:, at_j] = expo
        dprobs_ref[:, at_j] = dprobs


def merged(parts):
    largest = functools.reduce(jnp.maximum, [p[0:1] for p in parts])
    share = [jnp.exp2(p[0:1] - largest) for p in parts]
    total = sum(share)
    delta = sum(w * p[1:2] for w, p in zip(share, parts)) / total
    return largest + jnp.log2(total), delta


def backward_kernel(order, late, heads, shards, *refs):
    chunks = len(order)
    group, chunk = refs[:GROUP], refs[GROUP : GROUP + chunks]
    chunk = chunk[late[1] :] + chunk[late[0] : late[1]] + chunk[: late[0]]
    stats, refs = refs[GROUP + chunks :][:GROUP], refs[2 * GROUP + chunks :]
    (tops, expos, dprobs), refs = (refs[0:3], refs[3:6], refs[6:9]), refs[9:]
    near_ref, far_ref, *outs, dv_total, dk_total = refs
    rows, width = chunk[0].shape
    hd = width // 2
    shard = lax.axis_index("head")
    plane = lax.axis_index("ctx") // GROUP
    scaling = hd ** (-0.5)
    keys = jnp.concatenate([c[:, :hd] for c in chunk], axis=0)
    keys_across = keys.T
    for j in range(GROUP):
        at = pl.ds(j * heads * rows, heads * rows)
        parts = [
            s[0:2, pl.ds((j ^ t) * heads * rows, heads * rows)] for t, s in enumerate(stats)
        ]
        log_total, delta = merged(parts)
        weights = jnp.concatenate(
            [e[:, at] * jnp.exp2(t[0:1, at] - log_total) for e, t in zip(expos, tops)], axis=0
        )
        differences = jnp.concatenate([d[:, at] for d in dprobs], axis=0) - delta
        weights_low = weights.astype(jnp.bfloat16)
        dscores = (weights * differences).astype(jnp.bfloat16)
        dv = dot(weights_low, both_heads(group[j], heads, 1), NN)
        dk = dot(dscores, both_heads(group[j], heads, 0), NN)
        if j == 0:
            dv_total[...] = dv
            dk_total[...] = dk
        else:
            dv_total[...] += dv
            dk_total[...] += dk
        dq = ((dot(keys_across, dscores, NN) * scaling).T).astype(jnp.bfloat16)
        half = GROUP // 2
        to = (near_ref, far_ref)[j // half]
        for h in range(heads):
            to[pl.ds(j % half * rows, rows), h * hd : (h + 1) * hd] = dq[h * rows : (h + 1) * rows]
    part = rows // shards
    half = chunks // 2
    for t in range(shards):
        owner = lax.rem(shard + t, shards)
        for b in range(chunks):
            came = lax.rem((plane ^ b) - plane + chunks, chunks)
            at = sum(jnp.where(came == k, order.index(k), 0) for k in range(chunks))
            at = pl.ds(pl.multiple_of(at * rows + owner * part, part), part)
            if b < half:
                out, to = outs[b], pl.ds(t * part, part)
            else:
                out, to = outs[half + t], pl.ds((b - half) * part, part)
            out[to, :hd] = (dk_total[at, :] * scaling).astype(jnp.bfloat16)
            out[to, hd:] = dv_total[at, :].astype(jnp.bfloat16)


def fold_kernel(*refs):
    total = refs[0][...].astype(jnp.float32)
    for ref in refs[1:-1]:
        total = total + ref[...].astype(jnp.float32)
    refs[-1][...] = total.astype(jnp.bfloat16)


def finish_kernel(owned_ref, *refs):
    *came, key_ref, value_ref = refs
    part, hd = key_ref.shape
    total = owned_ref[:part].astype(jnp.float32)
    for ref in came:
        total = total + ref[...].astype(jnp.float32)
    key_ref[...] = total[:, :hd].astype(jnp.bfloat16)
    value_ref[...] = total[:, hd:].astype(jnp.bfloat16)


def query_sum_kernel(pair_ref, other_ref, query_ref):
    rows = query_ref.shape[0]
    query = pair_ref[:rows].astype(jnp.float32) + other_ref[...].astype(jnp.float32)
    query_ref[...] = query.astype(jnp.bfloat16)


def local(queries, key_rows, value_rows, out_grad, doc_lengths, span_order):
    rows, width = queries.shape
    hd = key_rows.shape[1]
    heads = width // hd
    ctx_size, shards = lax.axis_size("ctx"), lax.axis_size("head")
    chunks = ctx_size // GROUP
    part = rows // shards
    group_bits, chunk_bits = offsets(ctx_size)

    def swap(x, bits):
        return lax.ppermute(x, "ctx", [(i, i ^ bits) for i in range(ctx_size)])

    def shift(x, by):
        return lax.ppermute(x, "ctx", [(i, (i - by) % ctx_size) for i in range(ctx_size)])

    def turn(x, by):
        return lax.ppermute(x, "head", [(i, (i + by) % shards) for i in range(shards)])

    vmem = pl.BlockSpec(memory_space=pltpu.VMEM)
    params = pltpu.CompilerParams(vmem_limit_bytes=40 * 1024 * 1024)
    small = pltpu.CompilerParams(vmem_limit_bytes=4 * 1024 * 1024)

    def array(shape, dtype=jnp.bfloat16):
        return jax.ShapeDtypeStruct(shape, dtype)

    place = pl.pallas_call(
        functools.partial(place_kernel, group_bits, chunk_bits, doc_lengths.shape[0]),
        out_shape=array((2 * (GROUP + chunks), rows), jnp.int32),
        in_specs=[pl.BlockSpec(memory_space=pltpu.SMEM)],
        out_specs=vmem,
        compiler_params=small,
        cost_estimate=pl.CostEstimate(flops=10000000000, bytes_accessed=0, transcendentals=0),
        name="place",
    )(jnp.concatenate([doc_lengths, span_order.T.reshape(-1)]))

    packed = jnp.concatenate(
        [jnp.concatenate([key_rows, value_rows], axis=1), queries, out_grad], axis=0
    )
    packed = lax.optimization_barrier(packed)
    packed_kv, packed_qg = packed[:rows], packed[rows:]
    chunk = [packed_kv] + [shift(packed_kv, bits) for bits in chunk_bits[1:]]
    across = swap(packed_qg, group_bits[2])
    both = swap(jnp.concatenate([packed_qg, across], axis=0), group_bits[1])
    group = [packed_qg, both[: 2 * rows], across, both[2 * rows :]]

    last = tuple(range(1, chunks // 2))
    middle = tuple(range(chunks // 2, 3 * chunks // 4))
    late = middle + last
    early = (0, *range(3 * chunks // 4, chunks))

    def stats_of(which, before, flops):
        wide = array((len(which) * rows, GROUP * heads * rows), jnp.float32)
        return pl.pallas_call(
            functools.partial(stats_kernel, which, heads),
            out_shape=(
                array((2, GROUP * heads * rows), jnp.float32),
                array((1, GROUP * heads * rows), jnp.float32),
                wide,
                wide,
            ),
            in_specs=[vmem] * (1 + GROUP + len(which) + len(before)),
            out_specs=(vmem, vmem, vmem, vmem),
            compiler_params=params,
            cost_estimate=pl.CostEstimate(flops=flops, bytes_accessed=0, transcendentals=0),
            name="stats",
        )(place, *group, *[chunk[b] for b in which], *before)

    first, *kept_early = stats_of(early, (), 0)
    second, *kept_middle = stats_of(middle, (first,), 0)
    stats, *kept_last = stats_of(last, (second,), 0)
    kept = [ref for three in zip(kept_early, kept_middle, kept_last) for ref in three]
    all_stats = [stats] + [swap(stats, bits) for bits in group_bits[1:]]

    pair_rows = array((GROUP // 2 * rows, width))
    half = chunks // 2
    pieces = (array((rows, 2 * hd)),) * half + (array((half * part, 2 * hd)),) * shards
    near, far, *dkv = pl.pallas_call(
        functools.partial(backward_kernel, early + late, (len(last), len(late)), heads, shards),
        out_shape=(pair_rows, pair_rows) + pieces,
        in_specs=[vmem] * (2 * GROUP + chunks + len(kept)),
        out_specs=(vmem,) * (2 + len(pieces)),
        scratch_shapes=[pltpu.VMEM((chunks * rows, hd), jnp.float32)] * 2,
        compiler_params=params,
        name="backward",
    )(*group, *[chunk[b] for b in last + middle + early], *all_stats, *kept)

    def fold(parts, flops):
        return pl.pallas_call(
            fold_kernel,
            out_shape=jax.ShapeDtypeStruct(parts[0].shape, jnp.bfloat16),
            in_specs=[vmem] * len(parts),
            out_specs=vmem,
            compiler_params=small,
            cost_estimate=pl.CostEstimate(flops=flops, bytes_accessed=0, transcendentals=0),
            name="fold",
        )(*parts)

    across = fold([dkv[half]] + [turn(dkv[half + t], t) for t in range(1, shards)], 0)
    owned = fold([dkv[0]] + [swap(dkv[b], chunk_bits[b]) for b in range(1, half)], 1000000000)
    came = [
        swap(across[k * part : (k + 1) * part], chunk_bits[half + k]) for k in range(half)
    ] + [turn(owned[t * part : (t + 1) * part], t) for t in range(1, shards)]
    pair = (near.astype(jnp.float32) + swap(far, group_bits[2]).astype(jnp.float32)).astype(jnp.bfloat16)
    other = swap(pair[rows:], group_bits[1])
    query_grad = pl.pallas_call(
        query_sum_kernel,
        out_shape=array((rows, width)),
        in_specs=[vmem] * 2,
        out_specs=vmem,
        compiler_params=small,
        cost_estimate=pl.CostEstimate(flops=1000000000, bytes_accessed=0, transcendentals=0),
        name="query_sum",
    )(pair, other)
    query_grad, *came = lax.optimization_barrier((query_grad, *came))
    key_grad, value_grad = pl.pallas_call(
        finish_kernel,
        out_shape=(array((part, hd)), array((part, hd))),
        in_specs=[vmem] * (len(came) + 1),
        out_specs=(vmem, vmem),
        compiler_params=small,
        name="finish",
    )(owned, *came)
    return query_grad, key_grad, value_grad


def solution(mesh):
    in_specs = (P("ctx", "head"), P("ctx", None), P("ctx", None), P("ctx", "head"), P(), P())
    out_specs = (P("ctx", "head"), P(("ctx", "head"), None), P(("ctx", "head"), None))
    return jax.shard_map(local, mesh=mesh, in_specs=in_specs, out_specs=out_specs, check_vma=False)
```

```python
import functools

import jax
import jax.numpy as jnp
from jax import lax
from jax.experimental import pallas as pl
from jax.experimental.pallas import tpu as pltpu
from jax.sharding import PartitionSpec as P

masked_value = -1e30
log2_e = 1.4426950408889634
GROUP = 4

NT = (((1,), (1,)), ((), ()))
NN = (((1,), (0,)), ((), ()))


def dot(a, b, dims):
    return lax.dot_general(a, b, dims, preferred_element_type=jnp.float32)


def offsets(size):
    group = (0, 1, 2, 3)
    return group, tuple(range(0, size, GROUP))


def place_kernel(group, chunk, docs, ints, place_ref):
    rows = place_ref.shape[1]
    count = (ints.shape[0] - docs) // 2
    index = lax.axis_index("ctx")
    half = rows // 2
    at = lax.broadcasted_iota(jnp.int32, (1, rows), 1)
    for j, bits in enumerate(group):
        first = ints[docs + (index ^ bits)] * half
        second = ints[docs + count + (index ^ bits)] * half - half
        pos = at + jnp.where(at < half, first, second)
        start = jnp.int32(0)
        opens = jnp.zeros_like(pos)
        for d in range(docs):
            opens = jnp.where(pos >= start, start, opens)
            start = start + ints[d]
        place_ref[j : j + 1, :] = pos
        place_ref[GROUP + j : GROUP + j + 1, :] = opens
    for b, bits in enumerate(chunk):
        for h in range(2):
            to = 2 * GROUP + 2 * b + h
            origin = lax.rem(index + bits, count)
            base = ints[docs + h * count + origin] * half
            place_ref[to : to + 1, :] = jnp.full((1, rows), base)


def both_heads(ref, heads, which):
    rows, hd = ref.shape[0] // 2, ref.shape[1] // heads
    at = pl.ds(which * rows, rows)
    return jnp.concatenate([ref[at, h * hd : (h + 1) * hd] for h in range(heads)], axis=0)


def stats_kernel(which, heads, place_ref, *refs):
    count = len(which)
    group, chunk = refs[:GROUP], refs[GROUP : GROUP + count]
    *before, out_ref, top_ref, expo_ref, dprobs_ref = refs[GROUP + count :]
    rows, width = chunk[0].shape
    hd = width // 2
    factor = hd ** (-0.5) * log2_e
    keys = jnp.concatenate([c[:, :hd] for c in chunk], axis=0)
    values = jnp.concatenate([c[:, hd:] for c in chunk], axis=0)
    at = lax.broadcasted_iota(jnp.int32, (rows // 2, rows), 0)
    spans = [2 * (GROUP + b) + h for b in which for h in range(2)]
    key_pos = jnp.concatenate([at + place_ref[s : s + 1, :] for s in spans], axis=0)
    for j in range(GROUP):
        pos, opens = place_ref[j : j + 1, :], place_ref[GROUP + j : GROUP + j + 1, :]
        allowed = (key_pos <= pos) & (key_pos >= opens)
        bias = jnp.where(allowed, 0.0, masked_value)
        bias = jnp.concatenate([bias] * heads, axis=1)
        scores = dot(keys, both_heads(group[j], heads, 0), NT) * factor + bias
        dprobs = dot(values, both_heads(group[j], heads, 1), NT)
        top = jnp.max(scores, axis=0, keepdims=True)
        expo = jnp.exp2(scores - top)
        total = jnp.sum(expo, axis=0, keepdims=True)
        log_total = top + jnp.log2(total)
        delta = jnp.sum(expo * dprobs, axis=0, keepdims=True) / total
        at_j = pl.ds(j * heads * rows, heads * rows)
        if before:
            parts = [jnp.concatenate([log_total, delta], axis=0), before[0][:, at_j]]
            log_total, delta = merged(parts)
        out_ref[0:1, at_j] = log_total
        out_ref[1:2, at_j] = delta
        top_ref[0:1, at_j] = top
        expo_ref[:, at_j] = expo
        dprobs_ref[:, at_j] = dprobs


def merged(parts):
    largest = functools.reduce(jnp.maximum, [p[0:1] for p in parts])
    share = [jnp.exp2(p[0:1] - largest) for p in parts]
    total = sum(share)
    delta = sum(w * p[1:2] for w, p in zip(share, parts)) / total
    return largest + jnp.log2(total), delta


def backward_kernel(order, late, heads, shards, *refs):
    chunks = len(order)
    group, chunk = refs[:GROUP], refs[GROUP : GROUP + chunks]
    chunk = chunk[late[1] :] + chunk[late[0] : late[1]] + chunk[: late[0]]
    stats, refs = refs[GROUP + chunks :][:GROUP], refs[2 * GROUP + chunks :]
    (tops, expos, dprobs), refs = (refs[0:4], refs[4:8], refs[8:12]), refs[12:]
    near_ref, far_ref, *outs, dv_total, dk_total = refs
    rows, width = chunk[0].shape
    hd = width // 2
    shard = lax.axis_index("head")
    plane = lax.axis_index("ctx") // GROUP
    scaling = hd ** (-0.5)
    keys = jnp.concatenate([c[:, :hd] for c in chunk], axis=0)
    keys_across = keys.T
    for j in range(GROUP):
        at = pl.ds(j * heads * rows, heads * rows)
        parts = [
            s[0:2, pl.ds((j ^ t) * heads * rows, heads * rows)] for t, s in enumerate(stats)
        ]
        log_total, delta = merged(parts)
        weights = jnp.concatenate(
            [e[:, at] * jnp.exp2(t[0:1, at] - log_total) for e, t in zip(expos, tops)], axis=0
        )
        differences = jnp.concatenate([d[:, at] for d in dprobs], axis=0) - delta
        weights_low = weights.astype(jnp.bfloat16)
        dscores = (weights * differences).astype(jnp.bfloat16)
        dv = dot(weights_low, both_heads(group[j], heads, 1), NN)
        dk = dot(dscores, both_heads(group[j], heads, 0), NN)
        if j == 0:
            dv_total[...] = dv
            dk_total[...] = dk
        else:
            dv_total[...] += dv
            dk_total[...] += dk
        dq = ((dot(keys_across, dscores, NN) * scaling).T).astype(jnp.bfloat16)
        half = GROUP // 2
        to = (near_ref, far_ref)[j // half]
        for h in range(heads):
            to[pl.ds(j % half * rows, rows), h * hd : (h + 1) * hd] = dq[h * rows : (h + 1) * rows]
    part = rows // shards
    half = chunks // 2
    for t in range(shards):
        owner = lax.rem(shard + t, shards)
        for b in range(chunks):
            came = lax.rem((plane ^ b) - plane + chunks, chunks)
            at = sum(jnp.where(came == k, order.index(k), 0) for k in range(chunks))
            at = pl.ds(pl.multiple_of(at * rows + owner * part, part), part)
            if b < half:
                out, to = outs[b], pl.ds(t * part, part)
            else:
                out, to = outs[half + t], pl.ds((b - half) * part, part)
            out[to, :hd] = (dk_total[at, :] * scaling).astype(jnp.bfloat16)
            out[to, hd:] = dv_total[at, :].astype(jnp.bfloat16)


def fold_kernel(*refs):
    total = refs[0][...].astype(jnp.float32)
    for ref in refs[1:-1]:
        total = total + ref[...].astype(jnp.float32)
    refs[-1][...] = total.astype(jnp.bfloat16)


def finish_kernel(owned_ref, *refs):
    *came, key_ref, value_ref = refs
    part, hd = key_ref.shape
    total = owned_ref[:part].astype(jnp.float32)
    for ref in came:
        total = total + ref[...].astype(jnp.float32)
    key_ref[...] = total[:, :hd].astype(jnp.bfloat16)
    value_ref[...] = total[:, hd:].astype(jnp.bfloat16)


def query_sum_kernel(pair_ref, other_ref, query_ref):
    rows = query_ref.shape[0]
    query = pair_ref[:rows].astype(jnp.float32) + other_ref[...].astype(jnp.float32)
    query_ref[...] = query.astype(jnp.bfloat16)


def local(queries, key_rows, value_rows, out_grad, doc_lengths, span_order):
    rows, width = queries.shape
    hd = key_rows.shape[1]
    heads = width // hd
    ctx_size, shards = lax.axis_size("ctx"), lax.axis_size("head")
    chunks = ctx_size // GROUP
    part = rows // shards
    group_bits, chunk_bits = offsets(ctx_size)

    def swap(x, bits):
        return lax.ppermute(x, "ctx", [(i, i ^ bits) for i in range(ctx_size)])

    def shift(x, by):
        return lax.ppermute(x, "ctx", [(i, (i - by) % ctx_size) for i in range(ctx_size)])

    def turn(x, by):
        return lax.ppermute(x, "head", [(i, (i + by) % shards) for i in range(shards)])

    vmem = pl.BlockSpec(memory_space=pltpu.VMEM)
    params = pltpu.CompilerParams(vmem_limit_bytes=40 * 1024 * 1024)
    small = pltpu.CompilerParams(vmem_limit_bytes=4 * 1024 * 1024)

    def array(shape, dtype=jnp.bfloat16):
        return jax.ShapeDtypeStruct(shape, dtype)

    place = pl.pallas_call(
        functools.partial(place_kernel, group_bits, chunk_bits, doc_lengths.shape[0]),
        out_shape=array((2 * (GROUP + chunks), rows), jnp.int32),
        in_specs=[pl.BlockSpec(memory_space=pltpu.SMEM)],
        out_specs=vmem,
        compiler_params=small,
        cost_estimate=pl.CostEstimate(flops=10000000000, bytes_accessed=0, transcendentals=0),
        name="place",
    )(jnp.concatenate([doc_lengths, span_order.T.reshape(-1)]))

    packed = jnp.concatenate(
        [jnp.concatenate([key_rows, value_rows], axis=1), queries, out_grad], axis=0
    )
    packed = lax.optimization_barrier(packed)
    packed_kv, packed_qg = packed[:rows], packed[rows:]
    chunk = [packed_kv] + [shift(packed_kv, bits) for bits in chunk_bits[1:]]
    across = swap(packed_qg, group_bits[2])
    both = swap(jnp.concatenate([packed_qg, across], axis=0), group_bits[1])
    group = [packed_qg, both[: 2 * rows], across, both[2 * rows :]]

    last = tuple(range(1, chunks // 2))
    middle = tuple(range(chunks // 2, 3 * chunks // 4))
    late = middle + last
    early = (0, *range(3 * chunks // 4, chunks))

    def stats_of(which, before, flops):
        wide = array((len(which) * rows, GROUP * heads * rows), jnp.float32)
        return pl.pallas_call(
            functools.partial(stats_kernel, which, heads),
            out_shape=(
                array((2, GROUP * heads * rows), jnp.float32),
                array((1, GROUP * heads * rows), jnp.float32),
                wide,
                wide,
            ),
            in_specs=[vmem] * (1 + GROUP + len(which) + len(before)),
            out_specs=(vmem, vmem, vmem, vmem),
            compiler_params=params,
            cost_estimate=pl.CostEstimate(flops=flops, bytes_accessed=0, transcendentals=0),
            name="stats",
        )(place, *group, *[chunk[b] for b in which], *before)

    own, *kept_own = stats_of(early[:1], (), 0)
    first, *kept_early = stats_of(early[1:], (own,), 0)
    second, *kept_middle = stats_of(middle, (first,), 0)
    stats, *kept_last = stats_of(last, (second,), 0)
    kept = [ref for four in zip(kept_own, kept_early, kept_middle, kept_last) for ref in four]
    all_stats = [stats] + [swap(stats, bits) for bits in group_bits[1:]]

    pair_rows = array((GROUP // 2 * rows, width))
    half = chunks // 2
    pieces = (array((rows, 2 * hd)),) * half + (array((half * part, 2 * hd)),) * shards
    near, far, *dkv = pl.pallas_call(
        functools.partial(backward_kernel, early + late, (len(last), len(late)), heads, shards),
        out_shape=(pair_rows, pair_rows) + pieces,
        in_specs=[vmem] * (2 * GROUP + chunks + len(kept)),
        out_specs=(vmem,) * (2 + len(pieces)),
        scratch_shapes=[pltpu.VMEM((chunks * rows, hd), jnp.float32)] * 2,
        compiler_params=params,
        name="backward",
    )(*group, *[chunk[b] for b in last + middle + early], *all_stats, *kept)

    def fold(parts, flops):
        return pl.pallas_call(
            fold_kernel,
            out_shape=jax.ShapeDtypeStruct(parts[0].shape, jnp.bfloat16),
            in_specs=[vmem] * len(parts),
            out_specs=vmem,
            compiler_params=small,
            cost_estimate=pl.CostEstimate(flops=flops, bytes_accessed=0, transcendentals=0),
            name="fold",
        )(*parts)

    across = fold([dkv[half]] + [turn(dkv[half + t], t) for t in range(1, shards)], 0)
    owned = fold([dkv[0]] + [swap(dkv[b], chunk_bits[b]) for b in range(1, half)], 1000000000)
    came = [
        swap(across[k * part : (k + 1) * part], chunk_bits[half + k]) for k in range(half)
    ] + [turn(owned[t * part : (t + 1) * part], t) for t in range(1, shards)]
    pair = (near.astype(jnp.float32) + swap(far, group_bits[2]).astype(jnp.float32)).astype(jnp.bfloat16)
    other = swap(pair[rows:], group_bits[1])
    query_grad = pl.pallas_call(
        query_sum_kernel,
        out_shape=array((rows, width)),
        in_specs=[vmem] * 2,
        out_specs=vmem,
        compiler_params=small,
        cost_estimate=pl.CostEstimate(flops=1000000000, bytes_accessed=0, transcendentals=0),
        name="query_sum",
    )(pair, other)
    query_grad, *came = lax.optimization_barrier((query_grad, *came))
    key_grad, value_grad = pl.pallas_call(
        finish_kernel,
        out_shape=(array((part, hd)), array((part, hd))),
        in_specs=[vmem] * (len(came) + 1),
        out_specs=(vmem, vmem),
        compiler_params=small,
        name="finish",
    )(owned, *came)
    return query_grad, key_grad, value_grad


def solution(mesh):
    in_specs = (P("ctx", "head"), P("ctx", None), P("ctx", None), P("ctx", "head"), P(), P())
    out_specs = (P("ctx", "head"), P(("ctx", "head"), None), P(("ctx", "head"), None))
    return jax.shard_map(local, mesh=mesh, in_specs=in_specs, out_specs=out_specs, check_vma=False)
```
